128 devices in a mesh: rep: 8 (over x, core), graph: 16 (over y, z).
Axes of the slice: x: 4, y: 4, z: 4, core: 2. Of those that a mesh axis runs over, the one named last changes fastest.
Arguments:
- node_feats: bfloat16 [4096, 49, 128], P(('rep', 'graph')), may hold values from -6 to 6
- grad_out: bfloat16 [4096, 49, 128], P(('rep', 'graph')), may hold values from -6 to 6
- wigner: bfloat16 [235, 81920], P(None, ('rep', 'graph')), may hold values from -1.796875 to 1.796875
- weight_zero: bfloat16 [896, 896], replicated, may hold values from -0.1875 to 0.1875
- weight_one: bfloat16 [768, 2, 768], replicated, may hold values from -0.15625 to 0.15625
- weight_two: bfloat16 [640, 2, 640], replicated, may hold values from -0.15625 to 0.15625
- edge_source: int32 [81920], P(('rep', 'graph')), may hold values from 0 to 511
- edge_target: int32 [81920], P(('rep', 'graph')), may hold values from 0 to 31
- edge_count: int32 [128], P(('rep', 'graph')), may hold values from 320 to 640, as said below
Outputs:
- grad_feats: bfloat16 [4096, 49, 128], P(('rep', 'graph'))
- grad_zero: float32 [896, 896], P('graph')
- grad_one: float32 [768, 2, 768], P('graph')
- grad_two: float32 [640, 2, 640], P('graph')
The draws below stay inside these ranges and needn't reach their ends.
Inputs may be any that keep to these rules, and one draw needn't show every extreme that they name: `edge_count`: at least half of a device's 640 slots are live, and some device has all 640 live.
All inputs are finite; a program needn't handle non-finite values.
Results may differ from the reference program's by a relative error of at most 0.015.
Values may be sent and summed in bfloat16 or wider, within the bound.
No kernel may reach another device: no remote copies, remote signals or barrier semaphores. Data moves between devices by JAX's collectives and lax.ppermute only.
A program may use at most 192 MiB of HBM per device.

```python
import jax
import jax.numpy as jnp
from jax import lax

C = 128
LMAX = 6
ATOM_DEV = 32
EDGE_DEV = 640
ATOMS_GROUP = 512
ATOMS = 4096
EDGES = 81920
COEF = 49
ROT = 235
K0 = 896
K1 = 768
K2 = 640
N_REP = 8
N_GRAPH = 16


def draw_edge_count(key, part):
    key = jax.random.fold_in(key, 7)
    count_key, full_key = jax.random.split(key)
    device_total = N_REP * N_GRAPH
    counts = jax.random.randint(count_key, (device_total,), EDGE_DEV // 2, EDGE_DEV + 1)
    full_device = jax.random.randint(full_key, (), 0, device_total)
    return jnp.where(jnp.arange(device_total) == full_device, EDGE_DEV, counts).astype(jnp.int32)


def with_ends(entries, key, least, largest):
    dims = entries.shape
    spot = [jax.random.randint(jax.random.fold_in(key, axis), (), 0, dims[axis]) for axis in range(len(dims))]
    entries = entries.at[tuple(spot)].set(least)
    longest = dims.index(max(dims))
    spot[longest] = (spot[longest] + 1) % dims[longest]
    return entries.at[tuple(spot)].set(largest)


def level_of(own_key, dims, cuts, low, largest):
    def one(dim, blocks):
        draws = jax.random.uniform(jax.random.fold_in(jax.random.fold_in(own_key, 6), dim), (blocks,), jnp.float32, low / len(cuts), largest / len(cuts))
        return jnp.repeat(jnp.exp(draws), dims[dim] // blocks).reshape((-1,) + (1,) * (len(dims) - dim - 1))

    factor_of = one(*cuts[0])
    for cut in cuts[1:]:
        factor_of = factor_of * one(*cut)
    return factor_of


def scatter_about(key, extent, scale, limit, cuts=(), kind=jnp.bfloat16):
    array = jax.random.normal(key, extent, jnp.float32) * scale
    if len(cuts) > 0:
        array = level_of(key, extent, cuts, -0.22, 0.18) * array
    return jnp.clip(array, min=-limit, max=limit).astype(kind)


def setup_inputs(seed: int = 0) -> dict:
    keys = jax.random.split(jax.random.key(seed), 10)
    node_feats = scatter_about(keys[0], (ATOMS, COEF, C), 1.0, 6.0, ((0, 128),))
    grad_out = scatter_about(keys[1], (ATOMS, COEF, C), 1.0, 6.0, ((0, 128),))
    wigner = scatter_about(keys[2], (ROT, EDGES), 0.3, 1.796875, ((1, 128),))
    weight_zero = scatter_about(keys[3], (K0, K0), K0 ** -0.5, 0.1875)
    weight_one = scatter_about(keys[4], (K1, 2, K1), (2 * K1) ** -0.5, 0.15625)
    weight_two = scatter_about(keys[5], (K2, 2, K2), (2 * K2) ** -0.5, 0.15625)
    edge_source = with_ends(jax.random.randint(keys[6], (EDGES,), 0, ATOMS_GROUP), jax.random.fold_in(keys[6], 1), 0, ATOMS_GROUP - 1).astype(jnp.int32)
    edge_target = with_ends(jax.random.randint(keys[7], (EDGES,), 0, ATOM_DEV), jax.random.fold_in(keys[7], 1), 0, ATOM_DEV - 1).astype(jnp.int32)
    edge_count = draw_edge_count(jax.random.fold_in(keys[9], 71), 0)
    return {"node_feats": node_feats, "grad_out": grad_out, "wigner": wigner, "weight_zero": weight_zero, "weight_one": weight_one, "weight_two": weight_two, "edge_source": edge_source, "edge_target": edge_target, "edge_count": edge_count}


def dot_wide(left, right):
    return jnp.dot(left, right, preferred_element_type=jnp.float32)


def rotation_blocks(wigner, edge_total):
    blocks = []
    offset = 0
    for harmonic in range(LMAX + 1):
        kept_half = min(harmonic, 2)
        kept_rows = 2 * kept_half + 1
        full_rows = 2 * harmonic + 1
        rotation = wigner[offset:offset + kept_rows * full_rows].reshape(kept_rows, full_rows, edge_total)
        blocks.append(rotation.astype(jnp.float32))
        offset += kept_rows * full_rows
    return blocks


def to_frame(blocks, features):
    frame_parts = {azimuth: [] for azimuth in range(-2, 3)}
    for harmonic in range(LMAX + 1):
        kept_half = min(harmonic, 2)
        harmonic_rows = features[:, harmonic * harmonic:(harmonic + 1) ** 2, :].astype(jnp.float32)
        turned = jnp.einsum("rne,enc->erc", blocks[harmonic], harmonic_rows).astype(jnp.bfloat16)
        for azimuth in range(-kept_half, kept_half + 1):
            frame_parts[azimuth].append(turned[:, kept_half + azimuth, :])
    return {azimuth: jnp.concatenate(frame_parts[azimuth], axis=1) for azimuth in frame_parts}


def from_frame(blocks, frame_grads, channels):
    pieces = []
    for harmonic in range(LMAX + 1):
        kept_half = min(harmonic, 2)
        kept_slices = []
        for azimuth in range(-kept_half, kept_half + 1):
            position = harmonic - abs(azimuth)
            kept_slices.append(frame_grads[azimuth][:, position * channels:(position + 1) * channels])
        stacked = jnp.stack(kept_slices, axis=1).astype(jnp.float32)
        pieces.append(jnp.einsum("rne,erc->enc", blocks[harmonic], stacked).astype(jnp.bfloat16))
    return jnp.concatenate(pieces, axis=1)


def edge_grads(sources, cotangent, wigner, weight_zero, weight_one, weight_two):
    channels = sources.shape[2]
    blocks = rotation_blocks(wigner, sources.shape[0])
    frame_x = to_frame(blocks, sources)
    frame_g = to_frame(blocks, cotangent)
    grad_zero = dot_wide(frame_x[0].T, frame_g[0])
    frame_back = {0: dot_wide(frame_g[0], weight_zero.T).astype(jnp.bfloat16)}
    grad_pairs = []
    for azimuth, weights in ((1, weight_one), (2, weight_two)):
        real_part = weights[:, 0, :]
        imag_part = weights[:, 1, :]
        plus_x, minus_x = frame_x[azimuth], frame_x[-azimuth]
        plus_g, minus_g = frame_g[azimuth], frame_g[-azimuth]
        grad_real = dot_wide(plus_x.T, plus_g) + dot_wide(minus_x.T, minus_g)
        grad_imag = dot_wide(plus_x.T, minus_g) - dot_wide(minus_x.T, plus_g)
        grad_pairs.append(jnp.stack([grad_real, grad_imag], axis=1))
        frame_back[azimuth] = (dot_wide(plus_g, real_part.T) + dot_wide(minus_g, imag_part.T)).astype(jnp.bfloat16)
        frame_back[-azimuth] = (dot_wide(minus_g, real_part.T) - dot_wide(plus_g, imag_part.T)).astype(jnp.bfloat16)
    return from_frame(blocks, frame_back, channels), grad_zero, grad_pairs[0], grad_pairs[1]


def reference(node_feats, grad_out, wigner, weight_zero, weight_one, weight_two, edge_source, edge_target, edge_count):
    atom_total, coef_total, channels = node_feats.shape
    device_total = N_REP * N_GRAPH
    group_atoms = ATOM_DEV * N_GRAPH
    flat_x = node_feats.reshape(atom_total, coef_total * channels)
    flat_g = grad_out.reshape(atom_total, coef_total * channels)

    def visit_device(state_now, device_id):
        node_acc, acc_zero, acc_one, acc_two = state_now
        first_slot = (device_id * EDGE_DEV).astype(jnp.int32)
        local_source = lax.dynamic_slice_in_dim(edge_source, first_slot, EDGE_DEV)
        group_base = ((device_id // N_GRAPH) * group_atoms).astype(jnp.int32)
        source = local_source + group_base
        target = lax.dynamic_slice_in_dim(edge_target, first_slot, EDGE_DEV) + device_id * ATOM_DEV
        live_edges = (jnp.arange(EDGE_DEV, dtype=jnp.int32) < edge_count[device_id]).astype(jnp.bfloat16)
        sources = flat_x[source].reshape(EDGE_DEV, coef_total, channels)
        cotangent = (flat_g[target] * live_edges[:, None]).reshape(EDGE_DEV, coef_total, channels)
        rotation = lax.dynamic_slice_in_dim(wigner, first_slot, EDGE_DEV, 1)
        node_grad, grad_zero, grad_one, grad_two = edge_grads(sources, cotangent, rotation, weight_zero, weight_one, weight_two)
        partial_sum = jnp.zeros((group_atoms, coef_total * channels), jnp.float32)
        partial_sum = partial_sum.at[local_source].add(node_grad.reshape(EDGE_DEV, -1).astype(jnp.float32))
        rounded = lax.optimization_barrier(partial_sum.astype(jnp.bfloat16)).astype(jnp.float32)
        current = lax.dynamic_slice_in_dim(node_acc, group_base, group_atoms, 0)
        node_acc = lax.dynamic_update_slice_in_dim(node_acc, current + rounded, group_base, 0)
        return (node_acc, acc_zero + grad_zero, acc_one + grad_one, acc_two + grad_two), None

    initial = (jnp.zeros((atom_total, coef_total * channels), jnp.float32),
               jnp.zeros(weight_zero.shape, jnp.float32),
               jnp.zeros(weight_one.shape, jnp.float32),
               jnp.zeros(weight_two.shape, jnp.float32))
    final_state, _ = lax.scan(visit_device, initial, jnp.arange(device_total, dtype=jnp.int32))
    node_acc, acc_zero, acc_one, acc_two = final_state
    scale = float(device_total * EDGE_DEV) ** -0.5
    return (node_acc.astype(jnp.bfloat16).reshape(node_feats.shape), acc_zero * scale, acc_one * scale, acc_two * scale)
```

```python
import jax
import jax.numpy as jnp
from jax import lax
from jax.experimental import pallas as pl
from jax.experimental.pallas import tpu as pltpu
from jax.sharding import PartitionSpec as P

LMAX = 6
C = 128
PART_ROWS = 176
F32, BF16 = jnp.float32, jnp.bfloat16


def rot_offset(l):
    return sum((2 * min(i, 2) + 1) * (2 * i + 1) for i in range(l))


def rows_of(l):
    return 2 * min(l, 2) + 1


CH = 64


def turn(l, edges, rot_ref, in_ref, emit):
    kept, full, first = rows_of(l), 2 * l + 1, rot_offset(l)

    @pl.loop(0, edges // 128)
    def _(tile):
        e0 = pl.multiple_of(tile * 128, 128)
        for c0 in range(0, C, CH):
            acc = [None] * kept
            for n in range(full):
                x = in_ref[pl.ds(n * C + c0, CH), pl.ds(e0, 128)]
                for r in range(kept):
                    f = rot_ref[pl.ds(first + r * full + n, 1), pl.ds(e0, 128)]
                    t = f * x
                    acc[r] = t if acc[r] is None else acc[r] + t
            for r in range(kept):
                emit(r, c0, e0, acc[r])


def nt(a, b):
    return lax.dot_general(a, b, (((1,), (1,)), ((), ())), preferred_element_type=F32)


def tn(a, b):
    return lax.dot_general(a, b, (((0,), (0,)), ((), ())), preferred_element_type=F32)


def grad_kernel(count_ref, g_ref, wig_ref, w0_ref, w1_ref, w2_ref, src_ref, tgt_ref,
                g0_ref, g1_ref, g2_ref, part_ref,
                rot_ref, rows_ref, gv0_ref, gv1_ref, gv2_ref, gx_ref):
    edges = wig_ref.shape[1]
    atoms = g_ref.shape[1]
    parts = part_ref.shape[0]
    rot_ref[...] = wig_ref[...].astype(F32)
    slot = lax.broadcasted_iota(jnp.int32, (atoms, edges), 1)
    atom = lax.broadcasted_iota(jnp.int32, (atoms, edges), 0)
    chosen = jnp.where((tgt_ref[...] == atom) & (slot < count_ref[0]), 1.0, 0.0).astype(BF16)
    for l in range(LMAX + 1):
        kept, full = rows_of(l), 2 * l + 1
        half = kept // 2
        g = jnp.concatenate([g_ref[l * l + n] for n in range(full)], axis=1)
        rows_ref[: full * C, :] = tn(g, chosen)

        def emit(r, c0, e0, value, l=l, half=half):
            m = r - half
            v = value.astype(BF16)
            if m == 0:
                g0_ref[pl.ds(l * C + c0, CH), pl.ds(e0, 128)] = v
                return
            ref = g1_ref if abs(m) == 1 else g2_ref
            deep = ref.shape[0] // 2
            at = (l - abs(m)) * C + c0
            if m > 0:
                ref[pl.ds(at, CH), pl.ds(e0, 128)] = v
                ref[pl.ds(deep + at, CH), pl.ds(edges + e0, 128)] = -v
            else:
                ref[pl.ds(deep + at, CH), pl.ds(e0, 128)] = v
                ref[pl.ds(at, CH), pl.ds(edges + e0, 128)] = v

        turn(l, edges, rot_ref, rows_ref, emit)
    gv0_ref[...] = jnp.dot(w0_ref[...], g0_ref[...], preferred_element_type=F32).astype(BF16).astype(F32)
    for k in range(2):
        at = pl.ds(k * edges, edges)
        gv1_ref[:, at] = jnp.dot(w1_ref[...], g1_ref[:, at], preferred_element_type=F32).astype(BF16).astype(F32)
        gv2_ref[:, at] = jnp.dot(w2_ref[...], g2_ref[:, at], preferred_element_type=F32).astype(BF16).astype(F32)
    atom = lax.broadcasted_iota(jnp.int32, (parts * atoms, edges), 0)
    owners = jnp.where(src_ref[...] == atom, 1.0, 0.0).astype(BF16)
    for l in range(LMAX + 1):
        kept, full, first = rows_of(l), 2 * l + 1, rot_offset(l)
        half = kept // 2

        @pl.loop(0, edges // 128)
        def _(tile):
            e0 = pl.multiple_of(tile * 128, 128)
            for c0 in range(0, C, CH):
                s = []
                for r in range(kept):
                    m = r - half
                    ref = (gv0_ref, gv1_ref, gv2_ref)[abs(m)]
                    s.append(ref[pl.ds((l - abs(m)) * C + c0, CH), pl.ds((edges if m < 0 else 0) + e0, 128)])
                for n in range(full):
                    acc = None
                    for r in range(kept):
                        f = rot_ref[pl.ds(first + r * full + n, 1), pl.ds(e0, 128)]
                        t = f * s[r]
                        acc = t if acc is None else acc + t
                    gx_ref[pl.ds(n * C + c0, CH), pl.ds(e0, 128)] = acc.astype(BF16)

        out = nt(owners, gx_ref[: full * C, :]).astype(BF16)
        for n in range(full):
            part_ref[:, l * l + n] = out[:, n * C : (n + 1) * C].reshape(parts, atoms, C)


def weight_kernel(place_ref, x_ref, wig_ref, src_ref, g0_ref, g1_ref, g2_ref, mine0, mine1, mine2, mine3, their_ref,
                  rot_ref, rows_ref, v0_ref, v1_ref, v2_ref, slab_ref):
    mine_refs = (mine0, mine1, mine2, mine3)
    parts, _, atoms, _ = x_ref.shape
    edges = wig_ref.shape[1]
    rot_ref[...] = wig_ref[...].astype(F32)
    atom = lax.broadcasted_iota(jnp.int32, (parts * atoms, edges), 0)
    chosen = jnp.where(src_ref[...] == atom, 1.0, 0.0).astype(BF16)
    for l in range(LMAX + 1):
        kept, full = rows_of(l), 2 * l + 1
        half = kept // 2
        x = jnp.concatenate([x_ref[:, l * l + n].reshape(parts * atoms, C) for n in range(full)], axis=1)
        rows_ref[: full * C, :] = tn(x, chosen)

        def emit(r, c0, e0, value, l=l, half=half):
            m = r - half
            ref = (v0_ref, v1_ref, v2_ref)[abs(m)]
            ref[pl.ds((l - abs(m)) * C + c0, CH), pl.ds((edges if m < 0 else 0) + e0, 128)] = value.astype(BF16)

        turn(l, edges, rot_ref, rows_ref, emit)
    base = 0
    for v_ref, g_ref in ((v0_ref, g0_ref), (v1_ref, g1_ref), (v2_ref, g2_ref)):
        share = v_ref.shape[0] // parts
        width = g_ref.shape[0]
        for j in range(0, width, 256):
            wide = min(256, width - j)
            d = nt(v_ref[...], g_ref[j : j + wide, :])
            for k in range(0, wide, C):
                slab_ref[:, base : base + share, :] = d[:, k : k + C].reshape(parts, share, C)
                base += share
    slab_ref[:, base:, :] = jnp.zeros((parts, slab_ref.shape[1] - base, C), F32)
    part_rows = mine_refs[0].shape[1]
    x, core = place_ref[0], place_ref[1]
    for k in range(4):
        group = 2 * lax.rem(x + k, 4)
        at = pl.ds(pl.multiple_of((group + core) * part_rows, 8), part_rows)
        mine_refs[k][...] = slab_ref[:, at, :].astype(BF16)
        at = pl.ds(pl.multiple_of((group + 1 - core) * part_rows, 8), part_rows)
        their_ref[k] = slab_ref[:, at, :].astype(BF16)


VM = pl.BlockSpec(memory_space=pltpu.VMEM)
SM = pl.BlockSpec(memory_space=pltpu.SMEM)
S = jax.ShapeDtypeStruct


def grads(count, g, wig, w0, w1, w2, src, tgt, parts):
    coefs, atoms, _ = g.shape
    edges = wig.shape[1]
    rot = wig.shape[0]
    k0, k1, k2 = w0.shape[0], w1.shape[0], w2.shape[0]
    return pl.pallas_call(
        grad_kernel,
        out_shape=(S((k0, edges), BF16), S((2 * k1, 2 * edges), BF16), S((2 * k2, 2 * edges), BF16),
                   S((parts, coefs, atoms, C), BF16)),
        in_specs=[SM] + [VM] * 7,
        out_specs=[VM] * 4,
        scratch_shapes=[pltpu.VMEM((rot, edges), F32), pltpu.VMEM((13 * C, edges), F32),
                        pltpu.VMEM((k0, edges), F32), pltpu.VMEM((k1, 2 * edges), F32),
                        pltpu.VMEM((k2, 2 * edges), F32), pltpu.VMEM((13 * C, edges), BF16)],
        compiler_params=pltpu.CompilerParams(vmem_limit_bytes=60 << 20),
        name="grads",
    )(count, g, wig, w0, w1, w2, src, tgt)


def weights(place, x, wig, src, g0, g1, g2):
    edges = wig.shape[1]
    rot = wig.shape[0]
    parts = x.shape[0]
    k0, k1, k2 = g0.shape[0], g1.shape[0] // 2, g2.shape[0] // 2
    return pl.pallas_call(
        weight_kernel,
        out_shape=tuple(S((parts, PART_ROWS, C), BF16) for _ in range(4)) + (S((4, parts, PART_ROWS, C), BF16),),
        in_specs=[SM] + [VM] * 6,
        out_specs=[VM] * 5,
        scratch_shapes=[pltpu.VMEM((rot, edges), F32), pltpu.VMEM((13 * C, edges), F32),
                        pltpu.VMEM((k0, edges), BF16), pltpu.VMEM((k1, 2 * edges), BF16),
                        pltpu.VMEM((k2, 2 * edges), BF16), pltpu.VMEM((parts, 8 * PART_ROWS, C), F32)],
        compiler_params=pltpu.CompilerParams(vmem_limit_bytes=60 << 20),
        name="weights",
    )(place, x, wig, src, g0, g1, g2)


def graph_shift(dy, dz):
    return [(y * 4 + z, (y + dy) % 4 * 4 + (z + dz) % 4) for y in range(4) for z in range(4)]


def rep_shift(dx, dc):
    return [(x * 2 + c, (x + dx) % 4 * 2 + (c + dc) % 2) for x in range(4) for c in range(2)]


def send_rep(value, dx, dc):
    return lax.ppermute(value, "rep", rep_shift(dx, dc))


def add(*terms):
    total = terms[0].astype(F32)
    for t in terms[1:]:
        total = total + t.astype(F32)
    return total.astype(BF16)


def reduce_weights(mine, theirs):
    got = send_rep(theirs, 0, 1)
    r = [add(mine[k], got[k]) for k in range(4)]
    half = r[2].shape[0] // 2
    up = send_rep(r[2][:half], 1, 0)
    down = send_rep(r[2][half:], -1, 0)
    r1 = jnp.concatenate([add(r[1][:half], up), r[1][half:]])
    r3 = jnp.concatenate([r[3][:half], add(r[3][half:], down)])
    r0 = add(r[0], send_rep(r1, 1, 0), send_rep(r3, -1, 0))
    pieces = lax.all_to_all(r0, "graph", split_axis=0, concat_axis=0, tiled=True)
    total = pieces.astype(F32).sum(0)
    return lax.all_gather(total, "rep", axis=0, tiled=True)


def per_device(node_feats, grad_out, wigner, w0, w1, w2, edge_source, edge_target, edge_count):
    atoms, coefs, _ = node_feats.shape
    parts = lax.axis_size("graph")
    edges = edge_source.shape[0]
    x = lax.all_gather(node_feats.transpose(1, 0, 2), "graph", axis=0, tiled=False)
    src, tgt = edge_source[None], edge_target[None]
    g0, g1, g2, part = grads(
        edge_count, grad_out.transpose(1, 0, 2), wigner, w0, w1.reshape(w1.shape[0], -1), w2.reshape(w2.shape[0], -1), src, tgt, parts
    )
    grad_feats = lax.psum_scatter(part, "graph", scatter_dimension=0, tiled=False).transpose(1, 0, 2)
    rep = lax.axis_index("rep")
    place = jnp.stack([rep // 2, rep % 2])
    *mine, theirs = weights(place, x, wigner, src, g0, g1, g2)
    slab = reduce_weights(mine, theirs)
    scale = float(lax.axis_size("rep") * parts * edges) ** (-0.5)
    outs = []
    base = 0
    for w in (w0, w1, w2):
        share, tiles = w.shape[0] // parts, w[0].size // C
        rows = slab[base : base + share * tiles].reshape(tiles, share, C).transpose(1, 0, 2)
        outs.append(rows.reshape((share,) + w.shape[1:]) * scale)
        base += share * tiles
    return (grad_feats, *outs)


def solution(mesh):
    both = P(("rep", "graph"))
    edge_spec = P(("rep", "graph"))
    in_specs = (both, both, P(None, ("rep", "graph")), P(), P(), P(), edge_spec, edge_spec, edge_spec)
    out_specs = (both, P("graph"), P("graph"), P("graph"))
    return jax.shard_map(per_device, mesh=mesh, in_specs=in_specs, out_specs=out_specs, check_vma=False)
```

```python
import jax
import jax.numpy as jnp
from jax import lax
from jax.experimental import pallas as pl
from jax.experimental.pallas import tpu as pltpu
from jax.sharding import PartitionSpec as P

LMAX = 6
C = 128
PART_ROWS = 176
F32, BF16 = jnp.float32, jnp.bfloat16


def rot_offset(l):
    return sum((2 * min(i, 2) + 1) * (2 * i + 1) for i in range(l))


def rows_of(l):
    return 2 * min(l, 2) + 1


CH = 64


def turn(l, edges, rot_ref, in_ref, emit):
    kept, full, first = rows_of(l), 2 * l + 1, rot_offset(l)

    for tile in range(edges // 128):
        e0 = tile * 128
        for c0 in range(0, C, CH):
            acc = [None] * kept
            for n in range(full):
                x = in_ref[pl.ds(n * C + c0, CH), pl.ds(e0, 128)]
                for r in range(kept):
                    f = rot_ref[pl.ds(first + r * full + n, 1), pl.ds(e0, 128)]
                    t = f * x
                    acc[r] = t if acc[r] is None else acc[r] + t
            for r in range(kept):
                emit(r, c0, e0, acc[r])


def nt(a, b):
    return lax.dot_general(a, b, (((1,), (1,)), ((), ())), preferred_element_type=F32)


def tn(a, b):
    return lax.dot_general(a, b, (((0,), (0,)), ((), ())), preferred_element_type=F32)


def grad_kernel(count_ref, g_ref, wig_ref, w0_ref, w1_ref, w2_ref, src_ref, tgt_ref,
                g0_ref, g1_ref, g2_ref, part_ref,
                rot_ref, rows_ref, gv0_ref, gv1_ref, gv2_ref, gx_ref):
    edges = wig_ref.shape[1]
    atoms = g_ref.shape[1]
    parts = part_ref.shape[0]
    rot_ref[...] = wig_ref[...].astype(F32)
    slot = lax.broadcasted_iota(jnp.int32, (atoms, edges), 1)
    atom = lax.broadcasted_iota(jnp.int32, (atoms, edges), 0)
    chosen = jnp.where((tgt_ref[...] == atom) & (slot < count_ref[0]), 1.0, 0.0).astype(BF16)
    for l in range(LMAX + 1):
        kept, full = rows_of(l), 2 * l + 1
        half = kept // 2
        g = jnp.concatenate([g_ref[l * l + n] for n in range(full)], axis=1)
        rows_ref[: full * C, :] = tn(g, chosen)

        def emit(r, c0, e0, value, l=l, half=half):
            m = r - half
            v = value.astype(BF16)
            if m == 0:
                g0_ref[pl.ds(l * C + c0, CH), pl.ds(e0, 128)] = v
                return
            ref = g1_ref if abs(m) == 1 else g2_ref
            deep = ref.shape[0] // 2
            at = (l - abs(m)) * C + c0
            if m > 0:
                ref[pl.ds(at, CH), pl.ds(e0, 128)] = v
                ref[pl.ds(deep + at, CH), pl.ds(edges + e0, 128)] = -v
            else:
                ref[pl.ds(deep + at, CH), pl.ds(e0, 128)] = v
                ref[pl.ds(at, CH), pl.ds(edges + e0, 128)] = v

        turn(l, edges, rot_ref, rows_ref, emit)
    gv0_ref[...] = jnp.dot(w0_ref[...], g0_ref[...], preferred_element_type=F32).astype(BF16).astype(F32)
    for k in range(2):
        at = pl.ds(k * edges, edges)
        gv1_ref[:, at] = jnp.dot(w1_ref[...], g1_ref[:, at], preferred_element_type=F32).astype(BF16).astype(F32)
        gv2_ref[:, at] = jnp.dot(w2_ref[...], g2_ref[:, at], preferred_element_type=F32).astype(BF16).astype(F32)
    atom = lax.broadcasted_iota(jnp.int32, (parts * atoms, edges), 0)
    owners = jnp.where(src_ref[...] == atom, 1.0, 0.0).astype(BF16)
    for l in range(LMAX + 1):
        kept, full, first = rows_of(l), 2 * l + 1, rot_offset(l)
        half = kept // 2

        for tile in range(edges // 128):
            e0 = tile * 128
            for c0 in range(0, C, CH):
                s = []
                for r in range(kept):
                    m = r - half
                    ref = (gv0_ref, gv1_ref, gv2_ref)[abs(m)]
                    s.append(ref[pl.ds((l - abs(m)) * C + c0, CH), pl.ds((edges if m < 0 else 0) + e0, 128)])
                for n in range(full):
                    acc = None
                    for r in range(kept):
                        f = rot_ref[pl.ds(first + r * full + n, 1), pl.ds(e0, 128)]
                        t = f * s[r]
                        acc = t if acc is None else acc + t
                    gx_ref[pl.ds(n * C + c0, CH), pl.ds(e0, 128)] = acc.astype(BF16)

        out = nt(owners, gx_ref[: full * C, :]).astype(BF16)
        for n in range(full):
            part_ref[:, l * l + n] = out[:, n * C : (n + 1) * C].reshape(parts, atoms, C)


def weight_kernel(place_ref, x_ref, wig_ref, src_ref, g0_ref, g1_ref, g2_ref, mine0, mine1, mine2, mine3, their_ref,
                  rot_ref, rows_ref, v0_ref, v1_ref, v2_ref, slab_ref):
    mine_refs = (mine0, mine1, mine2, mine3)
    parts, _, atoms, _ = x_ref.shape
    edges = wig_ref.shape[1]
    rot_ref[...] = wig_ref[...].astype(F32)
    atom = lax.broadcasted_iota(jnp.int32, (parts * atoms, edges), 0)
    chosen = jnp.where(src_ref[...] == atom, 1.0, 0.0).astype(BF16)
    for l in range(LMAX + 1):
        kept, full = rows_of(l), 2 * l + 1
        half = kept // 2
        x = jnp.concatenate([x_ref[:, l * l + n].reshape(parts * atoms, C) for n in range(full)], axis=1)
        rows_ref[: full * C, :] = tn(x, chosen)

        def emit(r, c0, e0, value, l=l, half=half):
            m = r - half
            ref = (v0_ref, v1_ref, v2_ref)[abs(m)]
            ref[pl.ds((l - abs(m)) * C + c0, CH), pl.ds((edges if m < 0 else 0) + e0, 128)] = value.astype(BF16)

        turn(l, edges, rot_ref, rows_ref, emit)
    base = 0
    for v_ref, g_ref in ((v0_ref, g0_ref), (v1_ref, g1_ref), (v2_ref, g2_ref)):
        share = v_ref.shape[0] // parts
        width = g_ref.shape[0]
        for j in range(0, width, 256):
            wide = min(256, width - j)
            d = nt(v_ref[...], g_ref[j : j + wide, :])
            for k in range(0, wide, C):
                slab_ref[:, base : base + share, :] = d[:, k : k + C].reshape(parts, share, C)
                base += share
    slab_ref[:, base:, :] = jnp.zeros((parts, slab_ref.shape[1] - base, C), F32)
    part_rows = mine_refs[0].shape[1]
    x, core = place_ref[0], place_ref[1]
    for k in range(4):
        group = 2 * lax.rem(x + k, 4)
        at = pl.ds(pl.multiple_of((group + core) * part_rows, 8), part_rows)
        mine_refs[k][...] = slab_ref[:, at, :].astype(BF16)
        at = pl.ds(pl.multiple_of((group + 1 - core) * part_rows, 8), part_rows)
        their_ref[k] = slab_ref[:, at, :].astype(BF16)


VM = pl.BlockSpec(memory_space=pltpu.VMEM)
SM = pl.BlockSpec(memory_space=pltpu.SMEM)
S = jax.ShapeDtypeStruct


def grads(count, g, wig, w0, w1, w2, src, tgt, parts):
    coefs, atoms, _ = g.shape
    edges = wig.shape[1]
    rot = wig.shape[0]
    k0, k1, k2 = w0.shape[0], w1.shape[0], w2.shape[0]
    return pl.pallas_call(
        grad_kernel,
        out_shape=(S((k0, edges), BF16), S((2 * k1, 2 * edges), BF16), S((2 * k2, 2 * edges), BF16),
                   S((parts, coefs, atoms, C), BF16)),
        in_specs=[SM] + [VM] * 7,
        out_specs=[VM] * 4,
        scratch_shapes=[pltpu.VMEM((rot, edges), F32), pltpu.VMEM((13 * C, edges), F32),
                        pltpu.VMEM((k0, edges), F32), pltpu.VMEM((k1, 2 * edges), F32),
                        pltpu.VMEM((k2, 2 * edges), F32), pltpu.VMEM((13 * C, edges), BF16)],
        compiler_params=pltpu.CompilerParams(vmem_limit_bytes=60 << 20),
        name="grads",
    )(count, g, wig, w0, w1, w2, src, tgt)


def weights(place, x, wig, src, g0, g1, g2):
    edges = wig.shape[1]
    rot = wig.shape[0]
    parts = x.shape[0]
    k0, k1, k2 = g0.shape[0], g1.shape[0] // 2, g2.shape[0] // 2
    return pl.pallas_call(
        weight_kernel,
        out_shape=tuple(S((parts, PART_ROWS, C), BF16) for _ in range(4)) + (S((4, parts, PART_ROWS, C), BF16),),
        in_specs=[SM] + [VM] * 6,
        out_specs=[VM] * 5,
        scratch_shapes=[pltpu.VMEM((rot, edges), F32), pltpu.VMEM((13 * C, edges), F32),
                        pltpu.VMEM((k0, edges), BF16), pltpu.VMEM((k1, 2 * edges), BF16),
                        pltpu.VMEM((k2, 2 * edges), BF16), pltpu.VMEM((parts, 8 * PART_ROWS, C), F32)],
        compiler_params=pltpu.CompilerParams(vmem_limit_bytes=60 << 20),
        name="weights",
    )(place, x, wig, src, g0, g1, g2)


def graph_shift(dy, dz):
    return [(y * 4 + z, (y + dy) % 4 * 4 + (z + dz) % 4) for y in range(4) for z in range(4)]


def rep_shift(dx, dc):
    return [(x * 2 + c, (x + dx) % 4 * 2 + (c + dc) % 2) for x in range(4) for c in range(2)]


def send_rep(value, dx, dc):
    return lax.ppermute(value, "rep", rep_shift(dx, dc))


def add(*terms):
    total = terms[0].astype(F32)
    for t in terms[1:]:
        total = total + t.astype(F32)
    return total.astype(BF16)


def reduce_weights(mine, theirs):
    got = send_rep(theirs, 0, 1)
    r = [add(mine[k], got[k]) for k in range(4)]
    half = r[2].shape[0] // 2
    up = send_rep(r[2][:half], 1, 0)
    down = send_rep(r[2][half:], -1, 0)
    r1 = jnp.concatenate([add(r[1][:half], up), r[1][half:]])
    r3 = jnp.concatenate([r[3][:half], add(r[3][half:], down)])
    r0 = add(r[0], send_rep(r1, 1, 0), send_rep(r3, -1, 0))
    pieces = lax.all_to_all(r0, "graph", split_axis=0, concat_axis=0, tiled=True)
    total = pieces.astype(F32).sum(0)
    return lax.all_gather(total, "rep", axis=0, tiled=True)


def per_device(node_feats, grad_out, wigner, w0, w1, w2, edge_source, edge_target, edge_count):
    atoms, coefs, _ = node_feats.shape
    parts = lax.axis_size("graph")
    edges = edge_source.shape[0]
    x = lax.all_gather(node_feats.transpose(1, 0, 2), "graph", axis=0, tiled=False)
    src, tgt = edge_source[None], edge_target[None]
    g0, g1, g2, part = grads(
        edge_count, grad_out.transpose(1, 0, 2), wigner, w0, w1.reshape(w1.shape[0], -1), w2.reshape(w2.shape[0], -1), src, tgt, parts
    )
    grad_feats = lax.psum_scatter(part, "graph", scatter_dimension=0, tiled=False).transpose(1, 0, 2)
    rep = lax.axis_index("rep")
    place = jnp.stack([rep // 2, rep % 2])
    *mine, theirs = weights(place, x, wigner, src, g0, g1, g2)
    slab = reduce_weights(mine, theirs)
    scale = float(lax.axis_size("rep") * parts * edges) ** (-0.5)
    outs = []
    base = 0
    for w in (w0, w1, w2):
        share, tiles = w.shape[0] // parts, w[0].size // C
        rows = slab[base : base + share * tiles].reshape(tiles, share, C).transpose(1, 0, 2)
        outs.append(rows.reshape((share,) + w.shape[1:]) * scale)
        base += share * tiles
    return (grad_feats, *outs)


def solution(mesh):
    both = P(("rep", "graph"))
    edge_spec = P(("rep", "graph"))
    in_specs = (both, both, P(None, ("rep", "graph")), P(), P(), P(), edge_spec, edge_spec, edge_spec)
    out_specs = (both, P("graph"), P("graph"), P("graph"))
    return jax.shard_map(per_device, mesh=mesh, in_specs=in_specs, out_specs=out_specs, check_vma=False)
```

```python
import jax
import jax.numpy as jnp
from jax import lax
from jax.experimental import pallas as pl
from jax.experimental.pallas import tpu as pltpu
from jax.sharding import PartitionSpec as P

LMAX = 6
C = 128
FIRST_TILES = ((0, 5), (0, 6), (0, 5))
SECOND_TILES = ((5, 7), (6, 12), (5, 10))
FIRST_ROWS, SECOND_ROWS = 96, 80
F32, BF16 = jnp.float32, jnp.bfloat16


def rot_offset(l):
    return sum((2 * min(i, 2) + 1) * (2 * i + 1) for i in range(l))


def rows_of(l):
    return 2 * min(l, 2) + 1


CH = 64


def turn(l, edges, rot_ref, in_ref, emit):
    kept, full, first = rows_of(l), 2 * l + 1, rot_offset(l)

    for tile in range(edges // 128):
        e0 = tile * 128
        for c0 in range(0, C, CH):
            acc = [None] * kept
            for n in range(full):
                x = in_ref[pl.ds(n * C + c0, CH), pl.ds(e0, 128)]
                for r in range(kept):
                    f = rot_ref[pl.ds(first + r * full + n, 1), pl.ds(e0, 128)]
                    t = f * x
                    acc[r] = t if acc[r] is None else acc[r] + t
            for r in range(kept):
                emit(r, c0, e0, acc[r])


def nt(a, b):
    return lax.dot_general(a, b, (((1,), (1,)), ((), ())), preferred_element_type=F32)


def tn(a, b):
    return lax.dot_general(a, b, (((0,), (0,)), ((), ())), preferred_element_type=F32)


def grad_kernel(count_ref, g_ref, wig_ref, w0_ref, w1_ref, w2_ref, src_ref, tgt_ref,
                g0_ref, g1_ref, g2_ref, part_ref,
                rot_ref, rows_ref, gv0_ref, gv1_ref, gv2_ref, gx_ref):
    edges = wig_ref.shape[1]
    atoms = g_ref.shape[1]
    parts = part_ref.shape[0]
    rot_ref[...] = wig_ref[...].astype(F32)
    slot = lax.broadcasted_iota(jnp.int32, (atoms, edges), 1)
    atom = lax.broadcasted_iota(jnp.int32, (atoms, edges), 0)
    chosen = jnp.where((tgt_ref[...] == atom) & (slot < count_ref[0]), 1.0, 0.0).astype(BF16)
    for l in range(LMAX + 1):
        kept, full = rows_of(l), 2 * l + 1
        half = kept // 2
        g = jnp.concatenate([g_ref[l * l + n] for n in range(full)], axis=1)
        rows_ref[: full * C, :] = tn(g, chosen)

        def emit(r, c0, e0, value, l=l, half=half):
            m = r - half
            v = value.astype(BF16)
            if m == 0:
                g0_ref[pl.ds(l * C + c0, CH), pl.ds(e0, 128)] = v
                return
            ref = g1_ref if abs(m) == 1 else g2_ref
            deep = ref.shape[0] // 2
            at = (l - abs(m)) * C + c0
            if m > 0:
                ref[pl.ds(at, CH), pl.ds(e0, 128)] = v
                ref[pl.ds(deep + at, CH), pl.ds(edges + e0, 128)] = -v
            else:
                ref[pl.ds(deep + at, CH), pl.ds(e0, 128)] = v
                ref[pl.ds(at, CH), pl.ds(edges + e0, 128)] = v

        turn(l, edges, rot_ref, rows_ref, emit)
    gv0_ref[...] = jnp.dot(w0_ref[...], g0_ref[...], preferred_element_type=F32).astype(BF16).astype(F32)
    for k in range(2):
        at = pl.ds(k * edges, edges)
        gv1_ref[:, at] = jnp.dot(w1_ref[...], g1_ref[:, at], preferred_element_type=F32).astype(BF16).astype(F32)
        gv2_ref[:, at] = jnp.dot(w2_ref[...], g2_ref[:, at], preferred_element_type=F32).astype(BF16).astype(F32)
    atom = lax.broadcasted_iota(jnp.int32, (parts * atoms, edges), 0)
    owners = jnp.where(src_ref[...] == atom, 1.0, 0.0).astype(BF16)
    for l in range(LMAX + 1):
        kept, full, first = rows_of(l), 2 * l + 1, rot_offset(l)
        half = kept // 2

        for tile in range(edges // 128):
            e0 = tile * 128
            for c0 in range(0, C, CH):
                s = []
                for r in range(kept):
                    m = r - half
                    ref = (gv0_ref, gv1_ref, gv2_ref)[abs(m)]
                    s.append(ref[pl.ds((l - abs(m)) * C + c0, CH), pl.ds((edges if m < 0 else 0) + e0, 128)])
                for n in range(full):
                    acc = None
                    for r in range(kept):
                        f = rot_ref[pl.ds(first + r * full + n, 1), pl.ds(e0, 128)]
                        t = f * s[r]
                        acc = t if acc is None else acc + t
                    gx_ref[pl.ds(n * C + c0, CH), pl.ds(e0, 128)] = acc.astype(BF16)

        out = nt(owners, gx_ref[: full * C, :]).astype(BF16)
        for n in range(full):
            part_ref[:, l * l + n] = out[:, n * C : (n + 1) * C].reshape(parts, atoms, C)


def products(place_ref, v_refs, g_refs, tiles, slab_ref, mine_refs, their_ref):
    parts = slab_ref.shape[0]
    base = 0
    for v_ref, g_ref, (begin, end) in zip(v_refs, g_refs, tiles):
        share = v_ref.shape[0] // parts
        for j in range(begin * C, end * C, 256):
            wide = min(256, end * C - j)
            d = nt(v_ref[...], g_ref[j : j + wide, :])
            for k in range(0, wide, C):
                slab_ref[:, base : base + share, :] = d[:, k : k + C].reshape(parts, share, C)
                base += share
    if base < slab_ref.shape[1]:
        slab_ref[:, base:, :] = jnp.zeros((parts, slab_ref.shape[1] - base, C), F32)
    part_rows = mine_refs[0].shape[1]
    x, core = place_ref[0], place_ref[1]
    for k in range(4):
        group = 2 * lax.rem(x + k, 4)
        at = pl.ds(pl.multiple_of((group + core) * part_rows, 8), part_rows)
        mine_refs[k][...] = slab_ref[:, at, :].astype(BF16)
        at = pl.ds(pl.multiple_of((group + 1 - core) * part_rows, 8), part_rows)
        their_ref[k] = slab_ref[:, at, :].astype(BF16)


def first_kernel(place_ref, x_hbm, wig_ref, src_ref, g0_ref, g1_ref, g2_ref,
                 v0_ref, v1_ref, v2_ref, mine0, mine1, mine2, mine3, their_ref,
                 x_ref, sems, rot_ref, rows_ref, slab_ref):
    parts, _, atoms, _ = x_ref.shape
    edges = wig_ref.shape[1]
    copies = []
    for l in range(LMAX + 1):
        at = pl.ds(l * l, 2 * l + 1)
        copies.append(pltpu.make_async_copy(x_hbm.at[:, at], x_ref.at[:, at], sems.at[l]))
        copies[l].start()
    rot_ref[...] = wig_ref[...].astype(F32)
    atom = lax.broadcasted_iota(jnp.int32, (parts * atoms, edges), 0)
    chosen = jnp.where(src_ref[...] == atom, 1.0, 0.0).astype(BF16)
    for l in range(LMAX + 1):
        kept, full = rows_of(l), 2 * l + 1
        half = kept // 2
        copies[l].wait()
        x = jnp.concatenate([x_ref[:, l * l + n].reshape(parts * atoms, C) for n in range(full)], axis=1)
        rows_ref[: full * C, :] = tn(x, chosen)

        def emit(r, c0, e0, value, l=l, half=half):
            m = r - half
            ref = (v0_ref, v1_ref, v2_ref)[abs(m)]
            ref[pl.ds((l - abs(m)) * C + c0, CH), pl.ds((edges if m < 0 else 0) + e0, 128)] = value.astype(BF16)

        turn(l, edges, rot_ref, rows_ref, emit)
    products(place_ref, (v0_ref, v1_ref, v2_ref), (g0_ref, g1_ref, g2_ref), FIRST_TILES, slab_ref,
             (mine0, mine1, mine2, mine3), their_ref)


def second_kernel(place_ref, v0_ref, v1_ref, v2_ref, g0_ref, g1_ref, g2_ref,
                  mine0, mine1, mine2, mine3, their_ref, slab_ref):
    products(place_ref, (v0_ref, v1_ref, v2_ref), (g0_ref, g1_ref, g2_ref), SECOND_TILES, slab_ref,
             (mine0, mine1, mine2, mine3), their_ref)


VM = pl.BlockSpec(memory_space=pltpu.VMEM)
SM = pl.BlockSpec(memory_space=pltpu.SMEM)
ANY = pl.BlockSpec(memory_space=pl.ANY)
S = jax.ShapeDtypeStruct


def grads(count, g, wig, w0, w1, w2, src, tgt, parts):
    coefs, atoms, _ = g.shape
    edges = wig.shape[1]
    rot = wig.shape[0]
    k0, k1, k2 = w0.shape[0], w1.shape[0], w2.shape[0]
    return pl.pallas_call(
        grad_kernel,
        out_shape=(S((k0, edges), BF16), S((2 * k1, 2 * edges), BF16), S((2 * k2, 2 * edges), BF16),
                   S((parts, coefs, atoms, C), BF16)),
        in_specs=[SM] + [VM] * 7,
        out_specs=[VM] * 4,
        scratch_shapes=[pltpu.VMEM((rot, edges), F32), pltpu.VMEM((13 * C, edges), F32),
                        pltpu.VMEM((k0, edges), F32), pltpu.VMEM((k1, 2 * edges), F32),
                        pltpu.VMEM((k2, 2 * edges), F32), pltpu.VMEM((13 * C, edges), BF16)],
        compiler_params=pltpu.CompilerParams(vmem_limit_bytes=36 << 20),
        name="grads",
    )(count, g, wig, w0, w1, w2, src, tgt)


def sums(parts, rows):
    return tuple(S((parts, rows, C), BF16) for _ in range(4)) + (S((4, parts, rows, C), BF16),)


def first_weights(place, x, wig, src, g0, g1, g2):
    edges = wig.shape[1]
    rot = wig.shape[0]
    parts = x.shape[0]
    k0, k1, k2 = g0.shape[0], g1.shape[0] // 2, g2.shape[0] // 2
    return pl.pallas_call(
        first_kernel,
        out_shape=(S((k0, edges), BF16), S((k1, 2 * edges), BF16), S((k2, 2 * edges), BF16)) + sums(parts, FIRST_ROWS),
        in_specs=[SM, ANY] + [VM] * 5,
        out_specs=[VM] * 8,
        scratch_shapes=[pltpu.VMEM(x.shape, BF16), pltpu.SemaphoreType.DMA((LMAX + 1,)),
                        pltpu.VMEM((rot, edges), F32), pltpu.VMEM((13 * C, edges), F32),
                        pltpu.VMEM((parts, 8 * FIRST_ROWS, C), F32)],
        compiler_params=pltpu.CompilerParams(vmem_limit_bytes=40 << 20),
        cost_estimate=pl.CostEstimate(flops=10_000_000_000, bytes_accessed=20_000_000, transcendentals=0),
        name="first_weights",
    )(place, x, wig, src, g0, g1, g2)


def second_weights(place, v0, v1, v2, g0, g1, g2, parts):
    return pl.pallas_call(
        second_kernel,
        out_shape=sums(parts, SECOND_ROWS),
        in_specs=[SM] + [VM] * 6,
        out_specs=[VM] * 5,
        scratch_shapes=[pltpu.VMEM((parts, 8 * SECOND_ROWS, C), F32)],
        compiler_params=pltpu.CompilerParams(vmem_limit_bytes=32 << 20),
        cost_estimate=pl.CostEstimate(flops=4_000_000_000, bytes_accessed=10_000_000, transcendentals=0),
        name="second_weights",
    )(place, v0, v1, v2, g0, g1, g2)


def graph_shift(dy, dz):
    return [(y * 4 + z, (y + dy) % 4 * 4 + (z + dz) % 4) for y in range(4) for z in range(4)]


def rep_shift(dx, dc):
    return [(x * 2 + c, (x + dx) % 4 * 2 + (c + dc) % 2) for x in range(4) for c in range(2)]


def send_rep(value, dx, dc):
    return lax.ppermute(value, "rep", rep_shift(dx, dc))


def add(*terms):
    total = terms[0].astype(F32)
    for t in terms[1:]:
        total = total + t.astype(F32)
    return total.astype(BF16)


def sum_over_rep(mine, theirs):
    got = send_rep(theirs, 0, 1)
    r = [add(mine[k], got[k]) for k in range(4)]
    half = r[2].shape[0] // 2
    up = send_rep(r[2][:half], 1, 0)
    down = send_rep(r[2][half:], -1, 0)
    r1 = jnp.concatenate([add(r[1][:half], up), r[1][half:]])
    r3 = jnp.concatenate([r[3][:half], add(r[3][half:], down)])
    return add(r[0], send_rep(r1, 1, 0), send_rep(r3, -1, 0))


def per_device(node_feats, grad_out, wigner, w0, w1, w2, edge_source, edge_target, edge_count):
    atoms, coefs, _ = node_feats.shape
    parts = lax.axis_size("graph")
    edges = edge_source.shape[0]
    x = lax.all_gather(node_feats.transpose(1, 0, 2), "graph", axis=0, tiled=False)
    src, tgt = edge_source[None], edge_target[None]
    g0, g1, g2, part = grads(
        edge_count, grad_out.transpose(1, 0, 2), wigner, w0, w1.reshape(w1.shape[0], -1), w2.reshape(w2.shape[0], -1), src, tgt, parts
    )
    grad_feats = lax.psum_scatter(part, "graph", scatter_dimension=0, tiled=False).transpose(1, 0, 2)
    rep = lax.axis_index("rep")
    place = jnp.stack([rep // 2, rep % 2])
    v0, v1, v2, *mine, theirs = first_weights(place, x, wigner, src, g0, g1, g2)
    first = sum_over_rep(mine, theirs)
    *mine, theirs = second_weights(place, v0, v1, v2, g0, g1, g2, parts)
    second = sum_over_rep(mine, theirs)
    pieces = lax.all_to_all(jnp.concatenate([first, second], axis=1), "graph", split_axis=0, concat_axis=0, tiled=True)
    whole = lax.all_gather(pieces.astype(F32).sum(0), "rep", axis=0, tiled=False)
    first = whole[:, :FIRST_ROWS].reshape(-1, C)
    second = whole[:, FIRST_ROWS:].reshape(-1, C)
    scale = float(lax.axis_size("rep") * parts * edges) ** (-0.5)
    outs = []
    first_at = second_at = 0
    for w, early, late in zip((w0, w1, w2), FIRST_TILES, SECOND_TILES):
        share = w.shape[0] // parts
        n, k = (early[1] - early[0]) * share, (late[1] - late[0]) * share
        rows = jnp.concatenate([first[first_at : first_at + n], second[second_at : second_at + k]])
        first_at, second_at = first_at + n, second_at + k
        rows = rows.reshape(-1, share, C).transpose(1, 0, 2)
        outs.append(rows.reshape((share,) + w.shape[1:]) * scale)
    return (grad_feats, *outs)


def solution(mesh):
    both = P(("rep", "graph"))
    edge_spec = P(("rep", "graph"))
    in_specs = (both, both, P(None, ("rep", "graph")), P(), P(), P(), edge_spec, edge_spec, edge_spec)
    out_specs = (both, P("graph"), P("graph"), P("graph"))
    return jax.shard_map(per_device, mesh=mesh, in_specs=in_specs, out_specs=out_specs, check_vma=False)
```

```python
import jax
import jax.numpy as jnp
from jax import lax
from jax.experimental import pallas as pl
from jax.experimental.pallas import tpu as pltpu
from jax.sharding import PartitionSpec as P

LMAX = 6
C = 128
FIRST_TILES = ((0, 5), (0, 6), (0, 5))
SECOND_TILES = ((5, 7), (6, 12), (5, 10))
FIRST_ROWS, SECOND_ROWS = 96, 80
F32, BF16 = jnp.float32, jnp.bfloat16


def rot_offset(l):
    return sum((2 * min(i, 2) + 1) * (2 * i + 1) for i in range(l))


def rows_of(l):
    return 2 * min(l, 2) + 1


CH = 64
PARTS_STEP = 8


def turn(l, edges, rot_ref, in_ref, emit, loop=False):
    kept, full, first = rows_of(l), 2 * l + 1, rot_offset(l)

    def one(e0):
        for c0 in range(0, C, CH):
            acc = [None] * kept
            for n in range(full):
                x = in_ref[pl.ds(n * C + c0, CH), pl.ds(e0, 128)]
                for r in range(kept):
                    f = rot_ref[pl.ds(first + r * full + n, 1), pl.ds(e0, 128)]
                    t = f * x
                    acc[r] = t if acc[r] is None else acc[r] + t
            for r in range(kept):
                emit(r, c0, e0, acc[r])

    if loop:

        @pl.loop(0, edges // 128)
        def _(tile):
            one(pl.multiple_of(tile * 128, 128))
    else:
        for tile in range(edges // 128):
            one(tile * 128)


def nt(a, b):
    return lax.dot_general(a, b, (((1,), (1,)), ((), ())), preferred_element_type=F32)


def tn(a, b):
    return lax.dot_general(a, b, (((0,), (0,)), ((), ())), preferred_element_type=F32)


def grad_kernel(count_ref, g_ref, wig_ref, w0_ref, w1_ref, w2_ref, src_ref, tgt_ref,
                g0_ref, g1_ref, g2_ref, part_ref,
                rot_ref, rows_ref, gv0_ref, gv1_ref, gv2_ref, gx_ref, own_ref):
    edges = wig_ref.shape[1]
    atoms = g_ref.shape[1]
    parts = part_ref.shape[0]
    rot_ref[...] = wig_ref[...].astype(F32)
    slot = lax.broadcasted_iota(jnp.int32, (atoms, edges), 1)
    atom = lax.broadcasted_iota(jnp.int32, (atoms, edges), 0)
    chosen = jnp.where((tgt_ref[...] == atom) & (slot < count_ref[0]), 1.0, 0.0).astype(BF16)
    for l in range(LMAX + 1):
        kept, full = rows_of(l), 2 * l + 1
        half = kept // 2
        g = jnp.concatenate([g_ref[l * l + n] for n in range(full)], axis=1)
        rows_ref[: full * C, :] = tn(g, chosen)

        def emit(r, c0, e0, value, l=l, half=half):
            m = r - half
            v = value.astype(BF16)
            if m == 0:
                g0_ref[pl.ds(l * C + c0, CH), pl.ds(e0, 128)] = v
                return
            ref = g1_ref if abs(m) == 1 else g2_ref
            deep = ref.shape[0] // 2
            at = (l - abs(m)) * C + c0
            if m > 0:
                ref[pl.ds(at, CH), pl.ds(e0, 128)] = v
                ref[pl.ds(deep + at, CH), pl.ds(edges + e0, 128)] = -v
            else:
                ref[pl.ds(deep + at, CH), pl.ds(e0, 128)] = v
                ref[pl.ds(at, CH), pl.ds(edges + e0, 128)] = v

        turn(l, edges, rot_ref, rows_ref, emit, True)
    gv0_ref[...] = jnp.dot(w0_ref[...], g0_ref[...], preferred_element_type=F32).astype(BF16).astype(F32)

    @pl.loop(0, 2)
    def _(k):
        at = pl.ds(pl.multiple_of(k * edges, 128), edges)
        gv1_ref[:, at] = jnp.dot(w1_ref[...], g1_ref[:, at], preferred_element_type=F32).astype(BF16).astype(F32)
        gv2_ref[:, at] = jnp.dot(w2_ref[...], g2_ref[:, at], preferred_element_type=F32).astype(BF16).astype(F32)
    atom = lax.broadcasted_iota(jnp.int32, (parts * atoms, edges), 0)
    own_ref[...] = jnp.where(src_ref[...] == atom, 1.0, 0.0).astype(BF16)
    for l in range(LMAX + 1):
        kept, full, first = rows_of(l), 2 * l + 1, rot_offset(l)
        half = kept // 2

        @pl.loop(0, edges // 128)
        def _(tile):
            e0 = pl.multiple_of(tile * 128, 128)
            for c0 in range(0, C, CH):
                s = []
                for r in range(kept):
                    m = r - half
                    ref = (gv0_ref, gv1_ref, gv2_ref)[abs(m)]
                    s.append(ref[pl.ds((l - abs(m)) * C + c0, CH), pl.ds((edges if m < 0 else 0) + e0, 128)])
                for n in range(full):
                    acc = None
                    for r in range(kept):
                        f = rot_ref[pl.ds(first + r * full + n, 1), pl.ds(e0, 128)]
                        t = f * s[r]
                        acc = t if acc is None else acc + t
                    gx_ref[pl.ds(n * C + c0, CH), pl.ds(e0, 128)] = acc.astype(BF16)


        @pl.loop(0, parts // PARTS_STEP)
        def _(step):
            rows = PARTS_STEP * atoms
            out = nt(own_ref[pl.ds(pl.multiple_of(step * rows, rows), rows), :], gx_ref[: full * C, :]).astype(BF16)
            for n in range(full):
                part_ref[pl.ds(step * PARTS_STEP, PARTS_STEP), l * l + n] = out[:, n * C : (n + 1) * C].reshape(
                    PARTS_STEP, atoms, C
                )


def products(place_ref, v_refs, g_refs, tiles, slab_ref, mine_refs, their_ref):
    parts = slab_ref.shape[0]
    base = 0
    for v_ref, g_ref, (begin, end) in zip(v_refs, g_refs, tiles):
        share = v_ref.shape[0] // parts
        for j in range(begin * C, end * C, 256):
            wide = min(256, end * C - j)
            d = nt(v_ref[...], g_ref[j : j + wide, :])
            for k in range(0, wide, C):
                slab_ref[:, base : base + share, :] = d[:, k : k + C].reshape(parts, share, C)
                base += share
    if base < slab_ref.shape[1]:
        slab_ref[:, base:, :] = jnp.zeros((parts, slab_ref.shape[1] - base, C), F32)
    part_rows = mine_refs[0].shape[1]
    x, core = place_ref[0], place_ref[1]
    for k in range(4):
        group = 2 * lax.rem(x + k, 4)
        at = pl.ds(pl.multiple_of((group + core) * part_rows, 8), part_rows)
        mine_refs[k][...] = slab_ref[:, at, :].astype(BF16)
        at = pl.ds(pl.multiple_of((group + 1 - core) * part_rows, 8), part_rows)
        their_ref[k] = slab_ref[:, at, :].astype(BF16)


def first_kernel(place_ref, x_hbm, g1_hbm, g2_hbm, wig_ref, src_ref, g0_ref,
                 v0_ref, v1_ref, v2_ref, mine0, mine1, mine2, mine3, their_ref,
                 x_ref, g1_ref, g2_ref, sems, rot_ref, rows_ref, slab_ref):
    parts, _, atoms, _ = x_ref.shape
    edges = wig_ref.shape[1]
    copies = []
    for l in range(LMAX + 1):
        at = pl.ds(l * l, 2 * l + 1)
        copies.append(pltpu.make_async_copy(x_hbm.at[:, at], x_ref.at[:, at], sems.at[l]))
        copies[l].start()
    for k, (hbm, ref) in enumerate(((g1_hbm, g1_ref), (g2_hbm, g2_ref))):
        copies.append(pltpu.make_async_copy(hbm, ref, sems.at[LMAX + 1 + k]))
        copies[-1].start()
    rot_ref[...] = wig_ref[...].astype(F32)
    atom = lax.broadcasted_iota(jnp.int32, (parts * atoms, edges), 0)
    chosen = jnp.where(src_ref[...] == atom, 1.0, 0.0).astype(BF16)
    for l in range(LMAX + 1):
        kept, full = rows_of(l), 2 * l + 1
        half = kept // 2
        copies[l].wait()
        x = jnp.concatenate([x_ref[:, l * l + n].reshape(parts * atoms, C) for n in range(full)], axis=1)
        rows_ref[: full * C, :] = tn(x, chosen)

        def emit(r, c0, e0, value, l=l, half=half):
            m = r - half
            ref = (v0_ref, v1_ref, v2_ref)[abs(m)]
            ref[pl.ds((l - abs(m)) * C + c0, CH), pl.ds((edges if m < 0 else 0) + e0, 128)] = value.astype(BF16)

        turn(l, edges, rot_ref, rows_ref, emit)
    for copy in copies[LMAX + 1 :]:
        copy.wait()
    products(place_ref, (v0_ref, v1_ref, v2_ref), (g0_ref, g1_ref, g2_ref), FIRST_TILES, slab_ref,
             (mine0, mine1, mine2, mine3), their_ref)


def second_kernel(place_ref, v0_ref, v1_ref, v2_ref, g0_ref, g1_ref, g2_ref,
                  mine0, mine1, mine2, mine3, their_ref, slab_ref):
    products(place_ref, (v0_ref, v1_ref, v2_ref), (g0_ref, g1_ref, g2_ref), SECOND_TILES, slab_ref,
             (mine0, mine1, mine2, mine3), their_ref)


VM = pl.BlockSpec(memory_space=pltpu.VMEM)
SM = pl.BlockSpec(memory_space=pltpu.SMEM)
ANY = pl.BlockSpec(memory_space=pltpu.HBM)
S = jax.ShapeDtypeStruct


def grads(count, g, wig, w0, w1, w2, src, tgt, parts):
    coefs, atoms, _ = g.shape
    edges = wig.shape[1]
    rot = wig.shape[0]
    k0, k1, k2 = w0.shape[0], w1.shape[0], w2.shape[0]
    return pl.pallas_call(
        grad_kernel,
        out_shape=(S((k0, edges), BF16), S((2 * k1, 2 * edges), BF16), S((2 * k2, 2 * edges), BF16),
                   S((parts, coefs, atoms, C), BF16)),
        in_specs=[SM] + [VM] * 7,
        out_specs=[VM] * 4,
        scratch_shapes=[pltpu.VMEM((rot, edges), F32), pltpu.VMEM((13 * C, edges), F32),
                        pltpu.VMEM((k0, edges), F32), pltpu.VMEM((k1, 2 * edges), F32),
                        pltpu.VMEM((k2, 2 * edges), F32), pltpu.VMEM((13 * C, edges), BF16),
                        pltpu.VMEM((parts * atoms, edges), BF16)],
        compiler_params=pltpu.CompilerParams(vmem_limit_bytes=36 << 20),
        name="grads",
    )(count, g, wig, w0, w1, w2, src, tgt)


def sums(parts, rows):
    return tuple(S((parts, rows, C), BF16) for _ in range(4)) + (S((4, parts, rows, C), BF16),)


def first_weights(place, x, wig, src, g0, g1, g2):
    edges = wig.shape[1]
    rot = wig.shape[0]
    parts = x.shape[0]
    k0, k1, k2 = g0.shape[0], g1.shape[0] // 2, g2.shape[0] // 2
    return pl.pallas_call(
        first_kernel,
        out_shape=(S((k0, edges), BF16), S((k1, 2 * edges), BF16), S((k2, 2 * edges), BF16)) + sums(parts, FIRST_ROWS),
        in_specs=[SM, ANY, ANY, ANY] + [VM] * 3,
        out_specs=[VM] * 8,
        scratch_shapes=[pltpu.VMEM(x.shape, BF16), pltpu.VMEM(g1.shape, BF16), pltpu.VMEM(g2.shape, BF16),
                        pltpu.SemaphoreType.DMA((LMAX + 3,)),
                        pltpu.VMEM((rot, edges), F32), pltpu.VMEM((13 * C, edges), F32),
                        pltpu.VMEM((parts, 8 * FIRST_ROWS, C), F32)],
        compiler_params=pltpu.CompilerParams(vmem_limit_bytes=40 << 20),
        cost_estimate=pl.CostEstimate(flops=10_000_000_000, bytes_accessed=20_000_000, transcendentals=0),
        name="first_weights",
    )(place, x, g1, g2, wig, src, g0)


def second_weights(place, v0, v1, v2, g0, g1, g2, parts):
    return pl.pallas_call(
        second_kernel,
        out_shape=sums(parts, SECOND_ROWS),
        in_specs=[SM] + [VM] * 6,
        out_specs=[VM] * 5,
        scratch_shapes=[pltpu.VMEM((parts, 8 * SECOND_ROWS, C), F32)],
        compiler_params=pltpu.CompilerParams(vmem_limit_bytes=32 << 20),
        cost_estimate=pl.CostEstimate(flops=4_000_000_000, bytes_accessed=10_000_000, transcendentals=0),
        name="second_weights",
    )(place, v0, v1, v2, g0, g1, g2)


def graph_shift(dy, dz):
    return [(y * 4 + z, (y + dy) % 4 * 4 + (z + dz) % 4) for y in range(4) for z in range(4)]


def rep_shift(dx, dc):
    return [(x * 2 + c, (x + dx) % 4 * 2 + (c + dc) % 2) for x in range(4) for c in range(2)]


def send_rep(value, dx, dc):
    return lax.ppermute(value, "rep", rep_shift(dx, dc))


def add(*terms):
    total = terms[0].astype(F32)
    for t in terms[1:]:
        total = total + t.astype(F32)
    return total.astype(BF16)


def sum_over_rep(mine, theirs):
    got = send_rep(theirs, 0, 1)
    r = [add(mine[k], got[k]) for k in range(4)]
    half = r[2].shape[0] // 2
    up = send_rep(r[2][:half], 1, 0)
    down = send_rep(r[2][half:], -1, 0)
    r1 = jnp.concatenate([add(r[1][:half], up), r[1][half:]])
    r3 = jnp.concatenate([r[3][:half], add(r[3][half:], down)])
    return add(r[0], send_rep(r1, 1, 0), send_rep(r3, -1, 0))


def per_device(node_feats, grad_out, wigner, w0, w1, w2, edge_source, edge_target, edge_count):
    atoms, coefs, _ = node_feats.shape
    parts = lax.axis_size("graph")
    edges = edge_source.shape[0]
    x = lax.all_gather(node_feats.transpose(1, 0, 2), "graph", axis=0, tiled=False)
    src, tgt = edge_source[None], edge_target[None]
    g0, g1, g2, part = grads(
        edge_count, grad_out.transpose(1, 0, 2), wigner, w0, w1.reshape(w1.shape[0], -1), w2.reshape(w2.shape[0], -1), src, tgt, parts
    )
    grad_feats = lax.psum_scatter(part, "graph", scatter_dimension=0, tiled=False).transpose(1, 0, 2)
    rep = lax.axis_index("rep")
    place = jnp.stack([rep // 2, rep % 2])
    v0, v1, v2, *mine, theirs = first_weights(place, x, wigner, src, g0, g1, g2)
    first = sum_over_rep(mine, theirs)
    *mine, theirs = second_weights(place, v0, v1, v2, g0, g1, g2, parts)
    second = sum_over_rep(mine, theirs)
    pieces = lax.all_to_all(jnp.concatenate([first, second], axis=1), "graph", split_axis=0, concat_axis=0, tiled=True)
    whole = lax.all_gather(pieces.astype(F32).sum(0), "rep", axis=0, tiled=False)
    first = whole[:, :FIRST_ROWS].reshape(-1, C)
    second = whole[:, FIRST_ROWS:].reshape(-1, C)
    scale = float(lax.axis_size("rep") * parts * edges) ** (-0.5)
    outs = []
    first_at = second_at = 0
    for w, early, late in zip((w0, w1, w2), FIRST_TILES, SECOND_TILES):
        share = w.shape[0] // parts
        n, k = (early[1] - early[0]) * share, (late[1] - late[0]) * share
        rows = jnp.concatenate([first[first_at : first_at + n], second[second_at : second_at + k]])
        first_at, second_at = first_at + n, second_at + k
        rows = rows.reshape(-1, share, C).transpose(1, 0, 2)
        outs.append(rows.reshape((share,) + w.shape[1:]) * scale)
    return (grad_feats, *outs)


def solution(mesh):
    both = P(("rep", "graph"))
    edge_spec = P(("rep", "graph"))
    in_specs = (both, both, P(None, ("rep", "graph")), P(), P(), P(), edge_spec, edge_spec, edge_spec)
    out_specs = (both, P("graph"), P("graph"), P("graph"))
    return jax.shard_map(per_device, mesh=mesh, in_specs=in_specs, out_specs=out_specs, check_vma=False)
```

```python
import jax
import jax.numpy as jnp
from jax import lax
from jax.experimental import pallas as pl
from jax.experimental.pallas import tpu as pltpu
from jax.sharding import PartitionSpec as P

LMAX = 6
C = 128
FIRST_TILES = ((0, 5), (0, 6), (0, 5))
SECOND_TILES = ((5, 7), (6, 12), (5, 10))
FIRST_ROWS, SECOND_ROWS = 96, 80
F32, BF16 = jnp.float32, jnp.bfloat16


def rot_offset(l):
    return sum((2 * min(i, 2) + 1) * (2 * i + 1) for i in range(l))


def rows_of(l):
    return 2 * min(l, 2) + 1


CH = 64
PARTS_STEP = 8


def turn(l, edges, rot_ref, in_ref, emit, loop=False):
    kept, full, first = rows_of(l), 2 * l + 1, rot_offset(l)

    def one(e0):
        for c0 in range(0, C, CH):
            acc = [None] * kept
            for n in range(full):
                x = in_ref[pl.ds(n * C + c0, CH), pl.ds(e0, 128)]
                for r in range(kept):
                    f = rot_ref[pl.ds(first + r * full + n, 1), pl.ds(e0, 128)]
                    t = f * x
                    acc[r] = t if acc[r] is None else acc[r] + t
            for r in range(kept):
                emit(r, c0, e0, acc[r])

    if loop:

        @pl.loop(0, edges // 128)
        def _(tile):
            one(pl.multiple_of(tile * 128, 128))
    else:
        for tile in range(edges // 128):
            one(tile * 128)


def nt(a, b):
    return lax.dot_general(a, b, (((1,), (1,)), ((), ())), preferred_element_type=F32)


def tn(a, b):
    return lax.dot_general(a, b, (((0,), (0,)), ((), ())), preferred_element_type=F32)


def grad_kernel(count_ref, g_ref, wig_ref, w0_ref, w1_ref, w2_ref, src_ref, tgt_ref,
                g0_ref, g1_ref, g2_ref, part_ref,
                rot_ref, rows_ref, gv0_ref, gv1_ref, gv2_ref, gx_ref, own_ref):
    edges = wig_ref.shape[1]
    atoms = g_ref.shape[1]
    parts = part_ref.shape[0]
    rot_ref[...] = wig_ref[...].astype(F32)
    slot = lax.broadcasted_iota(jnp.int32, (atoms, edges), 1)
    atom = lax.broadcasted_iota(jnp.int32, (atoms, edges), 0)
    chosen = jnp.where((tgt_ref[...] == atom) & (slot < count_ref[0]), 1.0, 0.0).astype(BF16)
    for l in range(LMAX + 1):
        kept, full = rows_of(l), 2 * l + 1
        half = kept // 2
        g = jnp.concatenate([g_ref[l * l + n] for n in range(full)], axis=1)
        rows_ref[: full * C, :] = tn(g, chosen)

        def emit(r, c0, e0, value, l=l, half=half):
            m = r - half
            v = value.astype(BF16)
            if m == 0:
                g0_ref[pl.ds(l * C + c0, CH), pl.ds(e0, 128)] = v
                return
            ref = g1_ref if abs(m) == 1 else g2_ref
            deep = ref.shape[0] // 2
            at = (l - abs(m)) * C + c0
            if m > 0:
                ref[pl.ds(at, CH), pl.ds(e0, 128)] = v
                ref[pl.ds(deep + at, CH), pl.ds(edges + e0, 128)] = -v
            else:
                ref[pl.ds(deep + at, CH), pl.ds(e0, 128)] = v
                ref[pl.ds(at, CH), pl.ds(edges + e0, 128)] = v

        turn(l, edges, rot_ref, rows_ref, emit, True)
    gv0_ref[...] = jnp.dot(w0_ref[...], g0_ref[...], preferred_element_type=F32).astype(BF16).astype(F32)

    @pl.loop(0, 2)
    def _(k):
        at = pl.ds(pl.multiple_of(k * edges, 128), edges)
        gv1_ref[:, at] = jnp.dot(w1_ref[...], g1_ref[:, at], preferred_element_type=F32).astype(BF16).astype(F32)
        gv2_ref[:, at] = jnp.dot(w2_ref[...], g2_ref[:, at], preferred_element_type=F32).astype(BF16).astype(F32)
    atom = lax.broadcasted_iota(jnp.int32, (parts * atoms, edges), 0)
    own_ref[...] = jnp.where(src_ref[...] == atom, 1.0, 0.0).astype(BF16)
    for l in range(LMAX + 1):
        kept, full, first = rows_of(l), 2 * l + 1, rot_offset(l)
        half = kept // 2

        @pl.loop(0, edges // 128)
        def _(tile):
            e0 = pl.multiple_of(tile * 128, 128)
            for c0 in range(0, C, CH):
                s = []
                for r in range(kept):
                    m = r - half
                    ref = (gv0_ref, gv1_ref, gv2_ref)[abs(m)]
                    s.append(ref[pl.ds((l - abs(m)) * C + c0, CH), pl.ds((edges if m < 0 else 0) + e0, 128)])
                for n in range(full):
                    acc = None
                    for r in range(kept):
                        f = rot_ref[pl.ds(first + r * full + n, 1), pl.ds(e0, 128)]
                        t = f * s[r]
                        acc = t if acc is None else acc + t
                    gx_ref[pl.ds(n * C + c0, CH), pl.ds(e0, 128)] = acc.astype(BF16)


        @pl.loop(0, parts // PARTS_STEP)
        def _(step):
            rows = PARTS_STEP * atoms
            out = nt(own_ref[pl.ds(pl.multiple_of(step * rows, rows), rows), :], gx_ref[: full * C, :]).astype(BF16)
            for n in range(full):
                part_ref[pl.ds(step * PARTS_STEP, PARTS_STEP), l * l + n] = out[:, n * C : (n + 1) * C].reshape(
                    PARTS_STEP, atoms, C
                )


def products(place_ref, v_refs, g_refs, tiles, slab_ref, mine_refs, their_ref):
    parts = slab_ref.shape[0]
    base = 0
    for v_ref, g_ref, (begin, end) in zip(v_refs, g_refs, tiles):
        share = v_ref.shape[0] // parts
        for j in range(begin * C, end * C, 256):
            wide = min(256, end * C - j)
            d = nt(v_ref[...], g_ref[j : j + wide, :])
            for k in range(0, wide, C):
                slab_ref[:, base : base + share, :] = d[:, k : k + C].reshape(parts, share, C)
                base += share
    if base < slab_ref.shape[1]:
        slab_ref[:, base:, :] = jnp.zeros((parts, slab_ref.shape[1] - base, C), F32)
    part_rows = mine_refs[0].shape[1]
    x, core = place_ref[0], place_ref[1]
    for k in range(4):
        group = 2 * lax.rem(x + k, 4)
        at = pl.ds(pl.multiple_of((group + core) * part_rows, 8), part_rows)
        mine_refs[k][...] = slab_ref[:, at, :].astype(BF16)
        at = pl.ds(pl.multiple_of((group + 1 - core) * part_rows, 8), part_rows)
        their_ref[k] = slab_ref[:, at, :].astype(BF16)


def first_kernel(place_ref, x_hbm, g1_hbm, g2_hbm, wig_ref, src_ref, g0_ref,
                 v0_ref, v1_ref, v2_ref, mine0, mine1, mine2, mine3, their_ref,
                 x_ref, g1_ref, g2_ref, sems, rot_ref, rows_ref, slab_ref):
    parts, _, atoms, _ = x_ref.shape
    edges = wig_ref.shape[1]
    copies = []
    for l in range(LMAX + 1):
        at = pl.ds(l * l, 2 * l + 1)
        copies.append(pltpu.make_async_copy(x_hbm.at[:, at], x_ref.at[:, at], sems.at[l]))
        copies[l].start()
    for k, (hbm, ref) in enumerate(((g1_hbm, g1_ref), (g2_hbm, g2_ref))):
        copies.append(pltpu.make_async_copy(hbm, ref, sems.at[LMAX + 1 + k]))
        copies[-1].start()
    rot_ref[...] = wig_ref[...].astype(F32)
    atom = lax.broadcasted_iota(jnp.int32, (parts * atoms, edges), 0)
    chosen = jnp.where(src_ref[...] == atom, 1.0, 0.0).astype(BF16)
    for l in range(LMAX + 1):
        kept, full = rows_of(l), 2 * l + 1
        half = kept // 2
        copies[l].wait()
        x = jnp.concatenate([x_ref[:, l * l + n].reshape(parts * atoms, C) for n in range(full)], axis=1)
        rows_ref[: full * C, :] = tn(x, chosen)

        def emit(r, c0, e0, value, l=l, half=half):
            m = r - half
            ref = (v0_ref, v1_ref, v2_ref)[abs(m)]
            ref[pl.ds((l - abs(m)) * C + c0, CH), pl.ds((edges if m < 0 else 0) + e0, 128)] = value.astype(BF16)

        turn(l, edges, rot_ref, rows_ref, emit)
    for copy in copies[LMAX + 1 :]:
        copy.wait()
    products(place_ref, (v0_ref, v1_ref, v2_ref), (g0_ref, g1_ref, g2_ref), FIRST_TILES, slab_ref,
             (mine0, mine1, mine2, mine3), their_ref)


def second_kernel(place_ref, v0_ref, v1_ref, v2_ref, g0_ref, g1_ref, g2_ref,
                  mine0, mine1, mine2, mine3, their_ref, slab_ref):
    products(place_ref, (v0_ref, v1_ref, v2_ref), (g0_ref, g1_ref, g2_ref), SECOND_TILES, slab_ref,
             (mine0, mine1, mine2, mine3), their_ref)


VM = pl.BlockSpec(memory_space=pltpu.VMEM)
SM = pl.BlockSpec(memory_space=pltpu.SMEM)
ANY = pl.BlockSpec(memory_space=pltpu.HBM)
S = jax.ShapeDtypeStruct


def grads(count, g, wig, w0, w1, w2, src, tgt, parts):
    coefs, atoms, _ = g.shape
    edges = wig.shape[1]
    rot = wig.shape[0]
    k0, k1, k2 = w0.shape[0], w1.shape[0], w2.shape[0]
    return pl.pallas_call(
        grad_kernel,
        out_shape=(S((k0, edges), BF16), S((2 * k1, 2 * edges), BF16), S((2 * k2, 2 * edges), BF16),
                   S((parts, coefs, atoms, C), BF16)),
        in_specs=[SM] + [VM] * 7,
        out_specs=[VM] * 4,
        scratch_shapes=[pltpu.VMEM((rot, edges), F32), pltpu.VMEM((13 * C, edges), F32),
                        pltpu.VMEM((k0, edges), F32), pltpu.VMEM((k1, 2 * edges), F32),
                        pltpu.VMEM((k2, 2 * edges), F32), pltpu.VMEM((13 * C, edges), BF16),
                        pltpu.VMEM((parts * atoms, edges), BF16)],
        compiler_params=pltpu.CompilerParams(vmem_limit_bytes=36 << 20),
        name="grads",
    )(count, g, wig, w0, w1, w2, src, tgt)


def sums(parts, rows):
    return tuple(S((parts, rows, C), BF16) for _ in range(4)) + (S((4, parts, rows, C), BF16),)


def first_weights(place, x, wig, src, g0, g1, g2):
    edges = wig.shape[1]
    rot = wig.shape[0]
    parts = x.shape[0]
    k0, k1, k2 = g0.shape[0], g1.shape[0] // 2, g2.shape[0] // 2
    return pl.pallas_call(
        first_kernel,
        out_shape=(S((k0, edges), BF16), S((k1, 2 * edges), BF16), S((k2, 2 * edges), BF16)) + sums(parts, FIRST_ROWS),
        in_specs=[SM, ANY, ANY, ANY] + [VM] * 3,
        out_specs=[VM] * 8,
        scratch_shapes=[pltpu.VMEM(x.shape, BF16), pltpu.VMEM(g1.shape, BF16), pltpu.VMEM(g2.shape, BF16),
                        pltpu.SemaphoreType.DMA((LMAX + 3,)),
                        pltpu.VMEM((rot, edges), F32), pltpu.VMEM((13 * C, edges), F32),
                        pltpu.VMEM((parts, 8 * FIRST_ROWS, C), F32)],
        compiler_params=pltpu.CompilerParams(vmem_limit_bytes=40 << 20),
        cost_estimate=pl.CostEstimate(flops=10_000_000_000, bytes_accessed=20_000_000, transcendentals=0),
        name="first_weights",
    )(place, x, g1, g2, wig, src, g0)


def second_weights(place, v0, v1, v2, g0, g1, g2, parts):
    return pl.pallas_call(
        second_kernel,
        out_shape=sums(parts, SECOND_ROWS),
        in_specs=[SM] + [VM] * 6,
        out_specs=[VM] * 5,
        scratch_shapes=[pltpu.VMEM((parts, 8 * SECOND_ROWS, C), F32)],
        compiler_params=pltpu.CompilerParams(vmem_limit_bytes=32 << 20),
        cost_estimate=pl.CostEstimate(flops=4_000_000_000, bytes_accessed=10_000_000, transcendentals=0),
        name="second_weights",
    )(place, v0, v1, v2, g0, g1, g2)


def graph_shift(dy, dz):
    return [(y * 4 + z, (y + dy) % 4 * 4 + (z + dz) % 4) for y in range(4) for z in range(4)]


def rep_shift(dx, dc):
    return [(x * 2 + c, (x + dx) % 4 * 2 + (c + dc) % 2) for x in range(4) for c in range(2)]


def send_rep(value, dx, dc):
    return lax.ppermute(value, "rep", rep_shift(dx, dc))


def add(*terms):
    total = terms[0].astype(F32)
    for t in terms[1:]:
        total = total + t.astype(F32)
    return total.astype(BF16)


def pass_kernel(*refs):
    pass


def once(value, after):
    return pl.pallas_call(
        pass_kernel, out_shape=S(value.shape, value.dtype), in_specs=[VM] * 2, out_specs=VM,
        input_output_aliases={0: 0}, compiler_params=pltpu.CompilerParams(vmem_limit_bytes=8 << 20), name="once",
    )(value, after[(0,) * (after.ndim - 2)][:16])


def over_cores(mine, theirs):
    got = send_rep(theirs, 0, 1)
    far = add(mine[2], got[2])
    half = far.shape[0] // 2
    return got, far[:half], far[half:]


def first_step(mine, got, low, high):
    up = send_rep(low, 1, 0)
    down = send_rep(high, -1, 0)
    half = up.shape[0]
    to_up = jnp.concatenate([add(mine[1][:half], got[1][:half], up), add(mine[1][half:], got[1][half:])])
    to_down = jnp.concatenate([add(mine[3][:half], got[3][:half]), add(mine[3][half:], got[3][half:], down)])
    return to_up, to_down


def last_step(mine, got, to_up, to_down):
    return add(mine[0], got[0], send_rep(to_up, 1, 0), send_rep(to_down, -1, 0))


def per_device(node_feats, grad_out, wigner, w0, w1, w2, edge_source, edge_target, edge_count):
    atoms, coefs, _ = node_feats.shape
    parts = lax.axis_size("graph")
    edges = edge_source.shape[0]
    x = lax.all_gather(node_feats.transpose(1, 0, 2), "graph", axis=0, tiled=False)
    src, tgt = edge_source[None], edge_target[None]
    g0, g1, g2, part = grads(
        edge_count, grad_out.transpose(1, 0, 2), wigner, w0, w1.reshape(w1.shape[0], -1), w2.reshape(w2.shape[0], -1), src, tgt, parts
    )
    grad_feats = lax.psum_scatter(part, "graph", scatter_dimension=0, tiled=False).transpose(1, 0, 2)
    rep = lax.axis_index("rep")
    place = jnp.stack([rep // 2, rep % 2])
    v0, v1, v2, *mine, theirs = first_weights(place, x, wigner, src, g0, g1, g2)
    got, low, high = over_cores(mine, theirs)
    *mine2, theirs2 = second_weights(place, v0, v1, v2, g0, g1, g2, parts)
    got2, low2, high2 = over_cores(mine2, once(theirs2, got))
    to_up, to_down = first_step(mine, got, low, high)
    to_up2, to_down2 = first_step(mine2, got2, low2, high2)
    first = last_step(mine, got, to_up, to_down)
    second = last_step(mine2, got2, to_up2, to_down2)
    pieces = lax.all_to_all(jnp.concatenate([first, second], axis=1), "graph", split_axis=0, concat_axis=0, tiled=True)
    whole = lax.all_gather(pieces.astype(F32).sum(0), "rep", axis=0, tiled=False)
    first = whole[:, :FIRST_ROWS].reshape(-1, C)
    second = whole[:, FIRST_ROWS:].reshape(-1, C)
    scale = float(lax.axis_size("rep") * parts * edges) ** (-0.5)
    outs = []
    first_at = second_at = 0
    for w, early, late in zip((w0, w1, w2), FIRST_TILES, SECOND_TILES):
        share = w.shape[0] // parts
        n, k = (early[1] - early[0]) * share, (late[1] - late[0]) * share
        rows = jnp.concatenate([first[first_at : first_at + n], second[second_at : second_at + k]])
        first_at, second_at = first_at + n, second_at + k
        rows = rows.reshape(-1, share, C).transpose(1, 0, 2)
        outs.append(rows.reshape((share,) + w.shape[1:]) * scale)
    return (grad_feats, *outs)


def solution(mesh):
    both = P(("rep", "graph"))
    edge_spec = P(("rep", "graph"))
    in_specs = (both, both, P(None, ("rep", "graph")), P(), P(), P(), edge_spec, edge_spec, edge_spec)
    out_specs = (both, P("graph"), P("graph"), P("graph"))
    return jax.shard_map(per_device, mesh=mesh, in_specs=in_specs, out_specs=out_specs, check_vma=False)
```

```python
import jax
import jax.numpy as jnp
from jax import lax
from jax.experimental import pallas as pl
from jax.experimental.pallas import tpu as pltpu
from jax.sharding import PartitionSpec as P

LMAX = 6
C = 128
FIRST_TILES = ((0, 5), (0, 6), (0, 5))
SECOND_TILES = ((5, 7), (6, 12), (5, 10))
FIRST_ROWS, SECOND_ROWS = 96, 80
F32, BF16 = jnp.float32, jnp.bfloat16


def rot_offset(l):
    return sum((2 * min(i, 2) + 1) * (2 * i + 1) for i in range(l))


def rows_of(l):
    return 2 * min(l, 2) + 1


CH = 64
FEW = 4
PARTS_STEP = 8


def turn(l, edges, rot_ref, in_ref, emit, loop=False):
    kept, full, first = rows_of(l), 2 * l + 1, rot_offset(l)

    def one(e0):
        for c0 in range(0, C, CH):
            acc = [None] * kept
            for n in range(full):
                x = in_ref[pl.ds(n * C + c0, CH), pl.ds(e0, 128)]
                for r in range(kept):
                    f = rot_ref[pl.ds(first + r * full + n, 1), pl.ds(e0, 128)]
                    t = f * x
                    acc[r] = t if acc[r] is None else acc[r] + t
            for r in range(kept):
                emit(r, c0, e0, acc[r])

    if loop:

        @pl.loop(0, edges // 128)
        def _(tile):
            one(pl.multiple_of(tile * 128, 128))
    else:
        for tile in range(edges // 128):
            one(tile * 128)


def nt(a, b):
    return lax.dot_general(a, b, (((1,), (1,)), ((), ())), preferred_element_type=F32)


def tn(a, b):
    return lax.dot_general(a, b, (((0,), (0,)), ((), ())), preferred_element_type=F32)


def grad_kernel(count_ref, g_ref, wig_ref, w0_ref, w1_ref, w2_ref, src_ref, tgt_ref,
                g0_ref, g1_ref, g2_ref, part_ref,
                rot_ref, rows_ref, gv0_ref, gv1_ref, gv2_ref, gx_ref, own_ref):
    edges = wig_ref.shape[1]
    atoms = g_ref.shape[1]
    parts = part_ref.shape[0]
    rot_ref[...] = wig_ref[...].astype(F32)
    slot = lax.broadcasted_iota(jnp.int32, (atoms, edges), 1)
    atom = lax.broadcasted_iota(jnp.int32, (atoms, edges), 0)
    chosen = jnp.where((tgt_ref[...] == atom) & (slot < count_ref[0]), 1.0, 0.0).astype(BF16)
    for l in range(LMAX + 1):
        kept, full = rows_of(l), 2 * l + 1
        half = kept // 2
        g = jnp.concatenate([g_ref[l * l + n] for n in range(full)], axis=1)
        rows_ref[: full * C, :] = tn(g, chosen)

        def emit(r, c0, e0, value, l=l, half=half):
            m = r - half
            v = value.astype(BF16)
            if m == 0:
                g0_ref[pl.ds(l * C + c0, CH), pl.ds(e0, 128)] = v
                return
            ref = g1_ref if abs(m) == 1 else g2_ref
            deep = ref.shape[0] // 2
            at = (l - abs(m)) * C + c0
            if m > 0:
                ref[pl.ds(at, CH), pl.ds(e0, 128)] = v
                ref[pl.ds(deep + at, CH), pl.ds(edges + e0, 128)] = -v
            else:
                ref[pl.ds(deep + at, CH), pl.ds(e0, 128)] = v
                ref[pl.ds(at, CH), pl.ds(edges + e0, 128)] = v

        turn(l, edges, rot_ref, rows_ref, emit, True)
    gv0_ref[...] = jnp.dot(w0_ref[...], g0_ref[...], preferred_element_type=F32).astype(BF16).astype(F32)

    @pl.loop(0, 2)
    def _(k):
        at = pl.ds(pl.multiple_of(k * edges, 128), edges)
        gv1_ref[:, at] = jnp.dot(w1_ref[...], g1_ref[:, at], preferred_element_type=F32).astype(BF16).astype(F32)
        gv2_ref[:, at] = jnp.dot(w2_ref[...], g2_ref[:, at], preferred_element_type=F32).astype(BF16).astype(F32)
    atom = lax.broadcasted_iota(jnp.int32, (parts * atoms, edges), 0)
    own_ref[...] = jnp.where(src_ref[...] == atom, 1.0, 0.0).astype(BF16)
    for l in range(LMAX + 1):
        kept, full, first = rows_of(l), 2 * l + 1, rot_offset(l)
        half = kept // 2

        @pl.loop(0, edges // 128)
        def _(tile):
            e0 = pl.multiple_of(tile * 128, 128)
            for c0 in range(0, C, CH):
                s = []
                for r in range(kept):
                    m = r - half
                    ref = (gv0_ref, gv1_ref, gv2_ref)[abs(m)]
                    s.append(ref[pl.ds((l - abs(m)) * C + c0, CH), pl.ds((edges if m < 0 else 0) + e0, 128)])
                for n in range(full):
                    acc = None
                    for r in range(kept):
                        f = rot_ref[pl.ds(first + r * full + n, 1), pl.ds(e0, 128)]
                        t = f * s[r]
                        acc = t if acc is None else acc + t
                    gx_ref[pl.ds(n * C + c0, CH), pl.ds(e0, 128)] = acc.astype(BF16)


        @pl.loop(0, parts // PARTS_STEP)
        def _(step):
            rows = PARTS_STEP * atoms
            out = nt(own_ref[pl.ds(pl.multiple_of(step * rows, rows), rows), :], gx_ref[: full * C, :]).astype(BF16)
            for n in range(full):
                part_ref[pl.ds(step * PARTS_STEP, PARTS_STEP), l * l + n] = out[:, n * C : (n + 1) * C].reshape(
                    PARTS_STEP, atoms, C
                )


def products(place_ref, v_refs, g_refs, tiles, slab_ref, mine_refs, their_ref):
    parts = slab_ref.shape[0]
    base = 0
    for v_ref, g_ref, (begin, end) in zip(v_refs, g_refs, tiles):
        share = v_ref.shape[0] // parts
        for j in range(begin * C, end * C, 256):
            wide = min(256, end * C - j)
            d = nt(v_ref[...], g_ref[j : j + wide, :])
            for k in range(0, wide, C):
                slab_ref[:, base : base + share, :] = d[:, k : k + C].reshape(parts, share, C)
                base += share
    if base < slab_ref.shape[1]:
        slab_ref[:, base:, :] = jnp.zeros((parts, slab_ref.shape[1] - base, C), F32)
    part_rows = mine_refs[0].shape[1]
    x, core = place_ref[0], place_ref[1]
    for k in range(4):
        group = 2 * lax.rem(x + k, 4)
        at = pl.ds(pl.multiple_of((group + core) * part_rows, 8), part_rows)
        mine_refs[k][...] = slab_ref[:, at, :].astype(BF16)
        at = pl.ds(pl.multiple_of((group + 1 - core) * part_rows, 8), part_rows)
        their_ref[k] = slab_ref[:, at, :].astype(BF16)


def first_kernel(place_ref, few_hbm, x_hbm, g1_hbm, g2_hbm, wig_ref, src_ref, g0_ref,
                 v0_ref, v1_ref, v2_ref, mine0, mine1, mine2, mine3, their_ref,
                 x_ref, g1_ref, g2_ref, sems, rot_ref, rows_ref, slab_ref):
    parts, _, atoms, _ = x_ref.shape
    edges = wig_ref.shape[1]
    copies = []
    for l in range(LMAX + 1):
        at = pl.ds(l * l, 2 * l + 1)
        held, start = (few_hbm, l * l) if l * l < FEW else (x_hbm, l * l - FEW)
        copies.append(pltpu.make_async_copy(held.at[:, pl.ds(start, 2 * l + 1)], x_ref.at[:, at], sems.at[l]))
        copies[l].start()
    for k, (hbm, ref) in enumerate(((g1_hbm, g1_ref), (g2_hbm, g2_ref))):
        copies.append(pltpu.make_async_copy(hbm, ref, sems.at[LMAX + 1 + k]))
        copies[-1].start()
    rot_ref[...] = wig_ref[...].astype(F32)
    atom = lax.broadcasted_iota(jnp.int32, (parts * atoms, edges), 0)
    chosen = jnp.where(src_ref[...] == atom, 1.0, 0.0).astype(BF16)
    for l in range(LMAX + 1):
        kept, full = rows_of(l), 2 * l + 1
        half = kept // 2
        copies[l].wait()
        x = jnp.concatenate([x_ref[:, l * l + n].reshape(parts * atoms, C) for n in range(full)], axis=1)
        rows_ref[: full * C, :] = tn(x, chosen)

        def emit(r, c0, e0, value, l=l, half=half):
            m = r - half
            ref = (v0_ref, v1_ref, v2_ref)[abs(m)]
            ref[pl.ds((l - abs(m)) * C + c0, CH), pl.ds((edges if m < 0 else 0) + e0, 128)] = value.astype(BF16)

        turn(l, edges, rot_ref, rows_ref, emit)
    for copy in copies[LMAX + 1 :]:
        copy.wait()
    products(place_ref, (v0_ref, v1_ref, v2_ref), (g0_ref, g1_ref, g2_ref), FIRST_TILES, slab_ref,
             (mine0, mine1, mine2, mine3), their_ref)


def second_kernel(place_ref, v0_ref, v1_ref, v2_ref, g0_ref, g1_ref, g2_ref,
                  mine0, mine1, mine2, mine3, their_ref, slab_ref):
    products(place_ref, (v0_ref, v1_ref, v2_ref), (g0_ref, g1_ref, g2_ref), SECOND_TILES, slab_ref,
             (mine0, mine1, mine2, mine3), their_ref)


VM = pl.BlockSpec(memory_space=pltpu.VMEM)
SM = pl.BlockSpec(memory_space=pltpu.SMEM)
ANY = pl.BlockSpec(memory_space=pltpu.HBM)
S = jax.ShapeDtypeStruct


def grads(count, g, wig, w0, w1, w2, src, tgt, parts):
    coefs, atoms, _ = g.shape
    edges = wig.shape[1]
    rot = wig.shape[0]
    k0, k1, k2 = w0.shape[0], w1.shape[0], w2.shape[0]
    return pl.pallas_call(
        grad_kernel,
        out_shape=(S((k0, edges), BF16), S((2 * k1, 2 * edges), BF16), S((2 * k2, 2 * edges), BF16),
                   S((parts, coefs, atoms, C), BF16)),
        in_specs=[SM] + [VM] * 7,
        out_specs=[VM] * 4,
        scratch_shapes=[pltpu.VMEM((rot, edges), F32), pltpu.VMEM((13 * C, edges), F32),
                        pltpu.VMEM((k0, edges), F32), pltpu.VMEM((k1, 2 * edges), F32),
                        pltpu.VMEM((k2, 2 * edges), F32), pltpu.VMEM((13 * C, edges), BF16),
                        pltpu.VMEM((parts * atoms, edges), BF16)],
        compiler_params=pltpu.CompilerParams(vmem_limit_bytes=36 << 20),
        name="grads",
    )(count, g, wig, w0, w1, w2, src, tgt)


def sums(parts, rows):
    return tuple(S((parts, rows, C), BF16) for _ in range(4)) + (S((4, parts, rows, C), BF16),)


def first_weights(place, few, x, wig, src, g0, g1, g2):
    edges = wig.shape[1]
    rot = wig.shape[0]
    parts = x.shape[0]
    k0, k1, k2 = g0.shape[0], g1.shape[0] // 2, g2.shape[0] // 2
    return pl.pallas_call(
        first_kernel,
        out_shape=(S((k0, edges), BF16), S((k1, 2 * edges), BF16), S((k2, 2 * edges), BF16)) + sums(parts, FIRST_ROWS),
        in_specs=[SM] + [ANY] * 4 + [VM] * 3,
        out_specs=[VM] * 8,
        scratch_shapes=[pltpu.VMEM((parts, FEW + x.shape[1]) + x.shape[2:], BF16), pltpu.VMEM(g1.shape, BF16), pltpu.VMEM(g2.shape, BF16),
                        pltpu.SemaphoreType.DMA((LMAX + 3,)),
                        pltpu.VMEM((rot, edges), F32), pltpu.VMEM((13 * C, edges), F32),
                        pltpu.VMEM((parts, 8 * FIRST_ROWS, C), F32)],
        compiler_params=pltpu.CompilerParams(vmem_limit_bytes=40 << 20),
        cost_estimate=pl.CostEstimate(flops=10_000_000_000, bytes_accessed=20_000_000, transcendentals=0),
        name="first_weights",
    )(place, few, x, g1, g2, wig, src, g0)


def second_weights(place, v0, v1, v2, g0, g1, g2, parts):
    return pl.pallas_call(
        second_kernel,
        out_shape=sums(parts, SECOND_ROWS),
        in_specs=[SM] + [VM] * 6,
        out_specs=[VM] * 5,
        scratch_shapes=[pltpu.VMEM((parts, 8 * SECOND_ROWS, C), F32)],
        compiler_params=pltpu.CompilerParams(vmem_limit_bytes=32 << 20),
        cost_estimate=pl.CostEstimate(flops=4_000_000_000, bytes_accessed=10_000_000, transcendentals=0),
        name="second_weights",
    )(place, v0, v1, v2, g0, g1, g2)


def graph_shift(dy, dz):
    return [(y * 4 + z, (y + dy) % 4 * 4 + (z + dz) % 4) for y in range(4) for z in range(4)]


def rep_shift(dx, dc):
    return [(x * 2 + c, (x + dx) % 4 * 2 + (c + dc) % 2) for x in range(4) for c in range(2)]


def send_rep(value, dx, dc):
    return lax.ppermute(value, "rep", rep_shift(dx, dc))


def add(*terms):
    total = terms[0].astype(F32)
    for t in terms[1:]:
        total = total + t.astype(F32)
    return total.astype(BF16)


def pass_kernel(*refs):
    pass


def once(value, after):
    return pl.pallas_call(
        pass_kernel, out_shape=S(value.shape, value.dtype), in_specs=[VM] * 2, out_specs=VM,
        input_output_aliases={0: 0}, compiler_params=pltpu.CompilerParams(vmem_limit_bytes=8 << 20), name="once",
    )(value, after[(0,) * (after.ndim - 2)][:16])


def over_cores(mine, theirs):
    got = send_rep(theirs, 0, 1)
    far = add(mine[2], got[2])
    half = far.shape[0] // 2
    return got, far[:half], far[half:]


def first_step(mine, got, low, high):
    up = send_rep(low, 1, 0)
    down = send_rep(high, -1, 0)
    half = up.shape[0]
    to_up = jnp.concatenate([add(mine[1][:half], got[1][:half], up), add(mine[1][half:], got[1][half:])])
    to_down = jnp.concatenate([add(mine[3][:half], got[3][:half]), add(mine[3][half:], got[3][half:], down)])
    return to_up, to_down


def last_step(mine, got, to_up, to_down):
    return add(mine[0], got[0], send_rep(to_up, 1, 0), send_rep(to_down, -1, 0))


def per_device(node_feats, grad_out, wigner, w0, w1, w2, edge_source, edge_target, edge_count):
    atoms, coefs, _ = node_feats.shape
    parts = lax.axis_size("graph")
    edges = edge_source.shape[0]
    own = node_feats.transpose(1, 0, 2)
    few = lax.all_gather(own[:FEW], "graph", axis=0, tiled=False)
    x = lax.all_gather(own[FEW:], "graph", axis=0, tiled=False)
    src, tgt = edge_source[None], edge_target[None]
    g0, g1, g2, part = grads(
        edge_count, grad_out.transpose(1, 0, 2), wigner, w0, w1.reshape(w1.shape[0], -1), w2.reshape(w2.shape[0], -1), src, tgt, parts
    )
    grad_feats = lax.psum_scatter(part, "graph", scatter_dimension=0, tiled=False).transpose(1, 0, 2)
    rep = lax.axis_index("rep")
    place = jnp.stack([rep // 2, rep % 2])
    v0, v1, v2, *mine, theirs = first_weights(place, few, x, wigner, src, g0, g1, g2)
    got, low, high = over_cores(mine, theirs)
    *mine2, theirs2 = second_weights(place, v0, v1, v2, g0, g1, g2, parts)
    got2, low2, high2 = over_cores(mine2, once(theirs2, got))
    to_up, to_down = first_step(mine, got, low, high)
    to_up2, to_down2 = first_step(mine2, got2, low2, high2)
    first = last_step(mine, got, to_up, to_down)
    second = last_step(mine2, got2, to_up2, to_down2)
    pieces = lax.all_to_all(jnp.concatenate([first, second], axis=1), "graph", split_axis=0, concat_axis=0, tiled=True)
    whole = lax.all_gather(pieces.astype(F32).sum(0), "rep", axis=0, tiled=False)
    first = whole[:, :FIRST_ROWS].reshape(-1, C)
    second = whole[:, FIRST_ROWS:].reshape(-1, C)
    scale = float(lax.axis_size("rep") * parts * edges) ** (-0.5)
    outs = []
    first_at = second_at = 0
    for w, early, late in zip((w0, w1, w2), FIRST_TILES, SECOND_TILES):
        share = w.shape[0] // parts
        n, k = (early[1] - early[0]) * share, (late[1] - late[0]) * share
        rows = jnp.concatenate([first[first_at : first_at + n], second[second_at : second_at + k]])
        first_at, second_at = first_at + n, second_at + k
        rows = rows.reshape(-1, share, C).transpose(1, 0, 2)
        outs.append(rows.reshape((share,) + w.shape[1:]) * scale)
    return (grad_feats, *outs)


def solution(mesh):
    both = P(("rep", "graph"))
    edge_spec = P(("rep", "graph"))
    in_specs = (both, both, P(None, ("rep", "graph")), P(), P(), P(), edge_spec, edge_spec, edge_spec)
    out_specs = (both, P("graph"), P("graph"), P("graph"))
    return jax.shard_map(per_device, mesh=mesh, in_specs=in_specs, out_specs=out_specs, check_vma=False)
```
